512 devices in a mesh: dp: 8 (over z_lo, core), ctx: 64 (over y, z_hi, x).
Axes of the slice: x: 4, y: 8, z: 8 (z_hi: 2, z_lo: 4; z = z_hi * 4 + z_lo), core: 2. Of those that a mesh axis runs over, the one named last changes fastest.
Arguments:
- token_ids: int32 [8, 16384], P('dp'), may hold values from 0 to 30527
- target_ids: int32 [8], replicated, may hold values from 0 to 127
- candidates: int32 [4], replicated, may hold values from 0 to 7
- embed_table: bfloat16 [1536, 30528], P('ctx'), may hold values from -6 to 6
- online_blocks: bfloat16 [64, 256, 256], P('ctx'), may hold values from -0.375 to 0.375
- online_across: bfloat16 [256, 64, 64], P('ctx'), may hold values from -0.75 to 0.75
- online_channel: bfloat16 [2, 4, 384, 384], P(None, None, 'dp'), may hold values from -0.3125 to 0.3125
- online_gain: bfloat16 [1536], replicated, may hold values from 0.099609375 to 1.8984375
- online_head: bfloat16 [1536, 128], P('dp'), may hold values from -2 to 2
- ref_blocks: bfloat16 [64, 256, 256], P('ctx'), may hold values from -0.375 to 0.375
- ref_across: bfloat16 [256, 64, 64], P('ctx'), may hold values from -0.75 to 0.75
- ref_channel: bfloat16 [2, 4, 384, 384], P(None, None, 'dp'), may hold values from -0.3125 to 0.3125
- ref_gain: bfloat16 [1536], replicated, may hold values from 0.099609375 to 1.8984375
- ref_head: bfloat16 [1536, 128], P('dp'), may hold values from -2 to 2
Outputs:
- online_out: bfloat16 [131072, 1536], P(('dp', 'ctx'))
- scores: float32 [8], replicated
- picked: float32 [4], replicated
The draws below stay inside these ranges and needn't reach their ends.
All inputs are finite; a program needn't handle non-finite values.
Results may differ from the reference program's by a relative error of at most 0.005.
Values may be sent and summed in bfloat16 or wider, within the bound.
A program may use at most 64 MiB of HBM per device.

```python
import math
import jax
import jax.numpy as jnp
import numpy as np
from jax import lax

D = 1536
BLOCK = 256
CNUM = 4
CBLK = 384
VOCAB = 30528
NCLASS = 128
PICK = 4
SEQLEN = 16384
NB = 64
TOKENS = 131072
N_DP = 8


def head_values(key, spread_top):
    values = jnp.clip(jax.random.normal(key, (D, NCLASS), jnp.float32), -6.0, 6.0) * (3.0 / D ** 0.5)
    column_key = jax.random.fold_in(key, 1)
    factors = jnp.exp(jax.random.uniform(column_key, (1, NCLASS), jnp.float32, 0.0, jnp.log(spread_top)))
    return jnp.clip(values * factors, -2.0, 2.0).astype(jnp.bfloat16)


def draw_online_head(key, part):
    key = jax.random.fold_in(key, 11)
    return head_values(key, 1.5)


def draw_ref_head(key, part):
    key = jax.random.fold_in(key, 23)
    return head_values(key, 1.5)


def with_ends(array, rng, low, largest):
    shape = array.shape
    place = [jax.random.randint(jax.random.fold_in(rng, axis), (), 0, shape[axis]) for axis in range(len(shape))]
    array = array.at[tuple(place)].set(low)
    longest = shape.index(max(shape))
    place[longest] = (place[longest] + 1) % shape[longest]
    return array.at[tuple(place)].set(largest)


def steps_of(rng, shape, cuts, smallest, top_value):
    def one(axis_at, blocks):
        draws = jax.random.uniform(jax.random.fold_in(jax.random.fold_in(rng, 6), axis_at), (blocks,), jnp.float32, smallest / len(cuts), top_value / len(cuts))
        return jnp.repeat(jnp.exp(draws), shape[axis_at] // blocks).reshape((-1,) + (1,) * (len(shape) - axis_at - 1))

    loudness = one(*cuts[0])
    for cut in cuts[1:]:
        loudness = loudness * one(*cut)
    return loudness


def rank_bounds(amount, lean):
    portions = [(1 << 20) // math.isqrt(standing ** lean) + 1 for standing in range(1, amount + 1)]
    width = 1 + sum(portions) // (1 << 30)
    return np.cumsum(np.array([max(1, weight // width) for weight in portions]))


def ranked_ids(rng, extent, number_of, slope):
    grid = rank_bounds(number_of, slope)
    ticket = jax.random.randint(jax.random.fold_in(rng, 1), extent, 0, int(grid[number_of - 1]))
    grade = jnp.searchsorted(jnp.asarray(grid, jnp.int32), ticket, side="right")
    return jax.random.permutation(jax.random.fold_in(rng, 2), number_of)[grade].astype(jnp.int32)


def scatter_about(own_key, extent, spread, limit, split=(), held_as=jnp.bfloat16):
    array = jax.random.normal(own_key, extent, jnp.float32) * spread
    if len(split) > 0:
        array = steps_of(own_key, extent, split, -0.22, 0.18) * array
    return jnp.clip(array, min=-limit, max=limit).astype(held_as)


def setup_inputs(seed: int = 0) -> dict:
    splits = jax.random.split(jax.random.key(seed), 15)
    token_ids = with_ends(ranked_ids(splits[0], (N_DP, SEQLEN), VOCAB, 2), jax.random.fold_in(splits[0], 3), 0, VOCAB - 1).astype(jnp.int32)
    target_ids = with_ends(jax.random.randint(splits[1], (N_DP,), 0, NCLASS), jax.random.fold_in(splits[1], 1), 0, NCLASS - 1).astype(jnp.int32)
    candidates = with_ends(jax.random.randint(splits[2], (PICK,), 0, N_DP), jax.random.fold_in(splits[2], 1), 0, N_DP - 1).astype(jnp.int32)
    embed_table = scatter_about(splits[3], (D, VOCAB), 1.0, 6.0, ((0, 64),))
    online_blocks = scatter_about(splits[4], (NB, BLOCK, BLOCK), BLOCK ** -0.5, 0.375, ((0, 64),))
    online_across = scatter_about(splits[5], (BLOCK, NB, NB), NB ** -0.5, 0.75, ((0, 64),))
    online_channel = scatter_about(splits[6], (2, CNUM, CBLK, CBLK), CBLK ** -0.5, 0.3125, ((2, 8),))
    online_gain = jnp.clip(1.0 + 0.18 * jax.random.normal(splits[7], (D,), jnp.float32), 0.099609375, 1.8984375).astype(jnp.bfloat16)
    online_head = draw_online_head(jax.random.fold_in(splits[14], 71), 0)
    ref_blocks = scatter_about(splits[9], (NB, BLOCK, BLOCK), BLOCK ** -0.5, 0.375, ((0, 64),))
    ref_across = scatter_about(splits[10], (BLOCK, NB, NB), NB ** -0.5, 0.75, ((0, 64),))
    ref_channel = scatter_about(splits[11], (2, CNUM, CBLK, CBLK), CBLK ** -0.5, 0.3125, ((2, 8),))
    ref_gain = jnp.clip(1.0 + 0.18 * jax.random.normal(splits[12], (D,), jnp.float32), 0.099609375, 1.8984375).astype(jnp.bfloat16)
    ref_head = draw_ref_head(jax.random.fold_in(splits[14], 71), 0)
    return {"token_ids": token_ids, "target_ids": target_ids, "candidates": candidates, "embed_table": embed_table, "online_blocks": online_blocks, "online_across": online_across, "online_channel": online_channel, "online_gain": online_gain, "online_head": online_head, "ref_blocks": ref_blocks, "ref_across": ref_across, "ref_channel": ref_channel, "ref_gain": ref_gain, "ref_head": ref_head}


def channel_gate(normed_h, channel):
    tok_rows = normed_h.shape[0]
    section_one = jnp.einsum('tki,kij->tkj', normed_h.reshape(tok_rows, CNUM, CBLK).astype(jnp.float32), channel[0].astype(jnp.float32)).astype(jnp.bfloat16)
    permuted = jnp.transpose(section_one, (0, 2, 1)).reshape(tok_rows, CNUM, CBLK).astype(jnp.float32)
    section_two = jnp.einsum('tki,kij->tkj', permuted, channel[1].astype(jnp.float32))
    return jax.nn.sigmoid(section_two.reshape(tok_rows, D))

def model_layer(embedded, blocks, across, channel, gain):
    xfloat = embedded.astype(jnp.float32)
    normed_h = (xfloat * lax.rsqrt(lax.optimization_barrier(jnp.mean(xfloat * xfloat, axis=-1, keepdims=True)) + 1e-06) * gain.astype(jnp.float32)).astype(jnp.bfloat16)
    within = jnp.einsum('aoi,aic->aoc', blocks.astype(jnp.float32), normed_h.reshape(NB, BLOCK, D).astype(jnp.float32)).astype(jnp.bfloat16)
    mixed_all = jnp.einsum('bqa,abc->qbc', across.astype(jnp.float32), within.astype(jnp.float32)).astype(jnp.bfloat16)
    gate = channel_gate(normed_h, channel)
    return (xfloat + mixed_all.reshape(SEQLEN, D).astype(jnp.float32) * gate).astype(jnp.bfloat16)

def reference(token_ids, target_ids, candidates, embed_table, online_blocks, online_across, online_channel, online_gain, online_head, ref_blocks, ref_across, ref_channel, ref_gain, ref_head):

    def per_sequence(id_row):
        embedded = jnp.take(embed_table, id_row, axis=1).T
        online_y = model_layer(embedded, online_blocks, online_across, online_channel, online_gain)
        frozen_y = model_layer(embedded, ref_blocks, ref_across, ref_channel, ref_gain)
        sums = jnp.stack([lax.optimization_barrier(jnp.sum(online_y.astype(jnp.float32), axis=0)), lax.optimization_barrier(jnp.sum(frozen_y.astype(jnp.float32), axis=0))])
        return (online_y, sums)
    hidden, totals = lax.map(per_sequence, token_ids)
    pooled = totals / SEQLEN
    normalized = pooled * lax.rsqrt(lax.optimization_barrier(jnp.mean(pooled * pooled, axis=-1, keepdims=True)) + 1e-06)
    head_all = jnp.stack([online_head, ref_head]).astype(jnp.float32)
    logits = jnp.einsum('nmd,mdc->nmc', normalized, head_all, precision=lax.Precision.HIGHEST)
    total_exp = jax.nn.logsumexp(logits, axis=-1)
    chosen = jnp.take_along_axis(logits, jnp.broadcast_to(target_ids.astype(jnp.int32)[:, None, None], (N_DP, 2, 1)), axis=2)[:, :, 0]
    losses = total_exp - chosen
    scores = losses[:, 0] - losses[:, 1]
    picked = scores[candidates.astype(jnp.int32)]
    return (hidden.reshape(TOKENS, D), scores, picked)
```

```python
import functools
import jax
import jax.numpy as jnp
from jax import lax
from jax.experimental import pallas as pl
from jax.experimental.pallas import tpu as pltpu
from jax.sharding import PartitionSpec as P

MESH = pl.DeviceIdType.MESH


def score_kernel(dims, sums_ref, head_ref, target_ref, loss_ref,
                 buf_y, buf_z, buf_d, buf_l, own_y, own_z, own_l,
                 send_y, recv_y, send_z, recv_z, send_d, recv_d, send_l, recv_l):
    n_y, n_z, n_d, seq_len, width = dims
    dp = lax.axis_index("dp")
    ctx = lax.axis_index("ctx")
    my_y, my_z = ctx // n_z, lax.rem(ctx, n_z)

    def y_peer(o):
        return (dp, lax.rem(my_y + o, n_y) * n_z + my_z)

    def z_peer(o):
        return (dp, my_y * n_z + lax.rem(my_z + o, n_z))

    def d_peer(o):
        return (lax.rem(dp + o, n_d), ctx)

    stages = ((y_peer, n_y), (z_peer, n_z), (d_peer, n_d))
    barrier = pltpu.get_barrier_semaphore()
    for peer, count in stages:
        for o in range(1, count):
            pl.semaphore_signal(barrier, inc=1, device_id=peer(o), device_id_type=MESH)
    pl.semaphore_wait(barrier, n_y + n_z + n_d - 3)

    def exchange(own, buf, send, recv, peer, me, count):
        copies = []
        for o in range(1, count):
            copy = pltpu.make_async_remote_copy(
                src_ref=own, dst_ref=buf.at[me], send_sem=send.at[o], recv_sem=recv.at[me],
                device_id=peer(o), device_id_type=MESH)
            copy.start()
            copies.append(copy)
        buf[me] = own[...]
        for o in range(1, count):
            slot = lax.rem(me + o, count)
            pltpu.make_async_remote_copy(
                src_ref=own, dst_ref=buf.at[slot], send_sem=send.at[o], recv_sem=recv.at[slot],
                device_id=peer(o), device_id_type=MESH).wait_recv()
        return copies

    copies = exchange(sums_ref, buf_y, send_y, recv_y, y_peer, my_y, n_y)
    total = buf_y[0]
    for j in range(1, n_y):
        total = total + buf_y[j]
    own_y[...] = total
    copies += exchange(own_y, buf_z, send_z, recv_z, z_peer, my_z, n_z)
    total = buf_z[0]
    for j in range(1, n_z):
        total = total + buf_z[j]
    own_z[...] = total / seq_len
    copies += exchange(own_z, buf_d, send_d, recv_d, d_peer, dp, n_d)
    half = width // 2
    mine = (lax.broadcasted_iota(jnp.int32, (n_d, 1), 0) == dp).astype(jnp.float32)
    lane = lax.broadcasted_iota(jnp.int32, (1, width), 1) < half
    rows, squares = [], []
    for n in range(n_d):
        block = buf_d[n]
        rows.append(jnp.sum(block * mine, axis=0, keepdims=True))
        square = jnp.sum(block * block, axis=0, keepdims=True)
        squares.append((jnp.sum(jnp.where(lane, square, 0.0), axis=1, keepdims=True),
                        jnp.sum(jnp.where(lane, 0.0, square), axis=1, keepdims=True)))
    features = n_d * half
    scale_on = lax.rsqrt(jnp.concatenate([s[0] for s in squares], axis=0) / features + 1e-06)
    scale_ref = lax.rsqrt(jnp.concatenate([s[1] for s in squares], axis=0) / features + 1e-06)
    scaled = jnp.concatenate(rows, axis=0) * jnp.where(lane, scale_on, scale_ref)
    own_l[...] = jnp.dot(scaled, head_ref[...], precision=lax.Precision.HIGHEST,
                         preferred_element_type=jnp.float32)
    copies += exchange(own_l, buf_l, send_l, recv_l, d_peer, dp, n_d)
    logits = buf_l[0]
    for j in range(1, n_d):
        logits = logits + buf_l[j]
    classes = logits.shape[1] // 2
    chosen_mask = lax.broadcasted_iota(jnp.int32, (n_d, classes), 1) == target_ref[...]
    losses = []
    for part in (logits[:, :classes], logits[:, classes:]):
        top = jnp.max(part, axis=1, keepdims=True)
        total_exp = jnp.log(jnp.sum(jnp.exp(part - top), axis=1, keepdims=True)) + top
        losses.append(total_exp - jnp.sum(jnp.where(chosen_mask, part, 0.0), axis=1, keepdims=True))
    loss_ref[...] = jnp.broadcast_to(losses[0] - losses[1], loss_ref.shape)
    for copy in copies:
        copy.wait_send()


def score_call(sums, head, target_ids, seq_len):
    n_d, n_ctx = lax.axis_size("dp"), lax.axis_size("ctx")
    n_z = 8 if n_ctx == 64 else 2
    n_y = n_ctx // n_z
    width, classes = head.shape
    dims = (n_y, n_z, n_d, seq_len, width)
    f32 = jnp.float32
    dma = pltpu.SemaphoreType.DMA
    loss = pl.pallas_call(
        functools.partial(score_kernel, dims),
        out_shape=jax.ShapeDtypeStruct((n_d, 128), f32),
        in_specs=[pl.BlockSpec(memory_space=pltpu.VMEM)] * 3,
        out_specs=pl.BlockSpec(memory_space=pltpu.VMEM),
        scratch_shapes=[
            pltpu.VMEM((n_y, n_d, width), f32), pltpu.VMEM((n_z, n_d, width), f32),
            pltpu.VMEM((n_d, n_d, width), f32), pltpu.VMEM((n_d, n_d, classes), f32),
            pltpu.VMEM((n_d, width), f32), pltpu.VMEM((n_d, width), f32),
            pltpu.VMEM((n_d, classes), f32),
            dma((n_y,)), dma((n_y,)), dma((n_z,)), dma((n_z,)),
            dma((n_d,)), dma((n_d,)), dma((n_d,)), dma((n_d,)),
        ],
        compiler_params=pltpu.CompilerParams(collective_id=1, has_side_effects=True),
        name="score",
    )(sums, head, target_ids.reshape(n_d, 1))
    return loss[:, 0]


def channel_gate(normed_h, channel):
    tok_rows = normed_h.shape[0]
    block_count = channel.shape[1]
    block_width = channel.shape[2]
    section_one = jnp.einsum(
        "tki,kij->tkj",
        normed_h.reshape(tok_rows, block_count, block_width),
        channel[0],
        preferred_element_type=jnp.float32,
    ).astype(jnp.bfloat16)
    section_one = section_one.reshape(
        tok_rows, block_count, block_count, block_width // block_count
    )
    factor_two = channel[1].reshape(
        block_count, block_width // block_count, block_count, block_width
    )
    section_two = jnp.einsum(
        "tkqj,qjko->tqo", section_one, factor_two, preferred_element_type=jnp.float32
    )
    return jax.nn.sigmoid(section_two.reshape(tok_rows, block_count * block_width))


def normed(tokens, gain):
    xfloat = tokens.astype(jnp.float32)
    scaled = (
        xfloat
        * lax.rsqrt(jnp.mean(xfloat * xfloat, axis=-1, keepdims=True) + 1e-06)
        * gain.astype(jnp.float32)
    )
    return scaled.astype(jnp.bfloat16)


def within_blocks(normed_h, blocks):
    block_size = blocks.shape[1]
    shaped = normed_h.reshape(blocks.shape[0], block_size, normed_h.shape[1])
    return jnp.einsum("aoi,aic->aoc", blocks, shaped, preferred_element_type=jnp.float32).astype(
        jnp.bfloat16
    )


def run_models(tokens, member_set):
    channel_stack = jnp.stack([member[2] for member in member_set])
    channel_sets = lax.all_gather(channel_stack, "dp", axis=3, tiled=True)
    normed_list = [normed(tokens, member[3]) for member in member_set]
    within = jnp.stack([within_blocks(normed_list[0], member_set[0][0])])
    columns = lax.all_to_all(within, "ctx", split_axis=2, concat_axis=1, tiled=True)
    mixed_cols = jnp.stack(
        [
            jnp.einsum(
                "bqa,abc->qbc", member_set[0][1], columns[0], preferred_element_type=jnp.float32
            ).astype(jnp.bfloat16)
        ]
    )
    returned = lax.all_to_all(mixed_cols, "ctx", split_axis=1, concat_axis=2, tiled=True)
    xfloat = tokens.astype(jnp.float32)
    gate = channel_gate(normed_list[0], channel_sets[0])
    mixed_rows = returned[0].reshape(tokens.shape).astype(jnp.float32)
    outputs = [(xfloat + mixed_rows * gate).astype(jnp.bfloat16)]
    return outputs


def body(
    token_ids,
    target_ids,
    candidates,
    embed_table,
    online_blocks,
    online_across,
    online_channel,
    online_gain,
    online_head,
    ref_blocks,
    ref_across,
    ref_channel,
    ref_gain,
    ref_head,
):
    looked_up = jnp.take(embed_table, token_ids[0], axis=1)
    features = lax.all_to_all(looked_up, "ctx", split_axis=1, concat_axis=0, tiled=True)
    tokens = features.T
    online = (online_blocks, online_across, online_channel, online_gain, online_head)
    frozen = (ref_blocks, ref_across, ref_channel, ref_gain, ref_head)
    batches = ((online,), (frozen,))
    results = []
    for member_set in batches:
        results.extend(run_models(tokens, member_set))
    n_seqs = lax.axis_size("dp")
    sums = jnp.stack([jnp.sum(output.astype(jnp.float32), axis=0) for output in results])
    part = sums.shape[1] // n_seqs
    sums = sums.reshape(2, n_seqs, part).transpose(1, 0, 2).reshape(n_seqs, 2 * part)
    zeros = jnp.zeros_like(online_head)
    head = jnp.concatenate(
        [jnp.concatenate([online_head, zeros], axis=1), jnp.concatenate([zeros, ref_head], axis=1)],
        axis=0,
    ).astype(jnp.float32)
    scores = score_call(sums, head, target_ids, token_ids.shape[1])
    pick_mask = (candidates[:, None] == jnp.arange(n_seqs, dtype=jnp.int32)[None]).astype(
        jnp.float32
    )
    picked = jnp.sum(pick_mask * scores[None], axis=1)
    return (results[0], scores, picked)


def solution(mesh):
    in_specs = (
        P("dp", None),
        P(),
        P(),
        P("ctx", None),
        P("ctx", None, None),
        P("ctx", None, None),
        P(None, None, "dp", None),
        P(),
        P("dp", None),
        P("ctx", None, None),
        P("ctx", None, None),
        P(None, None, "dp", None),
        P(),
        P("dp", None),
    )
    out_specs = (P(("dp", "ctx"), None), P(), P())
    return jax.shard_map(body, mesh=mesh, in_specs=in_specs, out_specs=out_specs, check_vma=False)
```

```python
import functools
import jax
import jax.numpy as jnp
from jax import lax
from jax.experimental import pallas as pl
from jax.experimental.pallas import tpu as pltpu
from jax.sharding import PartitionSpec as P

MESH = pl.DeviceIdType.MESH
F32 = jnp.float32
BF16 = jnp.bfloat16
HALF_TILE = 4


def dot(a, b):
    return jnp.dot(a, b, preferred_element_type=F32)


def iota(shape, axis):
    return lax.broadcasted_iota(jnp.int32, shape, axis)


class Place:
    def __init__(self, n_d, n_c):
        self.n_d, self.n_c = n_d, n_c
        self.n_x = 4 if n_c == 64 else 1
        self.n_y = n_c // (2 * self.n_x)
        self.n_w = 2 * self.n_x
        self.z_lo_size = n_d // 2
        self.z_size = 2 * self.z_lo_size
        self.dp, self.ctx = lax.axis_index("dp"), lax.axis_index("ctx")
        self.y, self.w = self.ctx // self.n_w, lax.rem(self.ctx, self.n_w)
        self.z_hi, self.x = self.w // self.n_x, lax.rem(self.w, self.n_x)
        self.z_lo, self.core = self.dp // 2, lax.rem(self.dp, 2)
        self.z = self.z_hi * self.z_lo_size + self.z_lo

    def ctx_at(self, o):
        step_y = lax.rem(lax.rem(o, self.n_y) * 3, self.n_y)
        rest = o // self.n_y
        step_z, step_x = lax.rem(rest, 2), rest // 2
        y = lax.rem(self.y + step_y, self.n_y)
        z_hi = lax.rem(self.z_hi + step_z, 2)
        x = lax.rem(self.x + step_x, self.n_x)
        return y * self.n_w + z_hi * self.n_x + x

    def z_at(self, step):
        z = lax.rem(self.z + step, self.z_size)
        dp = lax.rem(z, self.z_lo_size) * 2 + self.core
        ctx = self.y * self.n_w + (z // self.z_lo_size) * self.n_x + self.x
        return dp, ctx

    def y_peer(self, o):
        return (self.dp, lax.rem(self.y + o, self.n_y) * self.n_w + self.w)

    def w_peer(self, o):
        return (self.dp, self.y * self.n_w + lax.rem(self.w + o, self.n_w))

    def d_peer(self, o):
        return (lax.rem(self.dp + o, self.n_d), self.ctx)


def remote(src, dst, send, recv, device):
    return pltpu.make_async_remote_copy(
        src_ref=src, dst_ref=dst, send_sem=send, recv_sem=recv,
        device_id=device, device_id_type=MESH)


def exchange(own, buf, send, recv, peer, me, count):
    copies = []
    for o in range(1, count):
        copy = remote(own, buf.at[me], send.at[o], recv.at[me], peer(o))
        copy.start()
        copies.append(copy)
    buf[me] = own[...]
    for o in range(1, count):
        slot = lax.rem(me + o, count)
        remote(own, buf.at[slot], send.at[o], recv.at[slot], peer(o)).wait_recv()
    return copies


def total_of(buf, count):
    total = buf[0]
    for j in range(1, count):
        total = total + buf[j]
    return total


def to_chunks(parts, ref):
    rows, width = parts[0].shape
    tiles = [p.reshape(rows // 8, 8, width) for p in parts]
    rolled = [pltpu.roll(t, HALF_TILE, 1) for t in tiles]
    upper = iota((1, 8, 1), 1) < HALF_TILE
    even = [jnp.where(upper, tiles[i], rolled[i + 1]) for i in (0, 2)]
    odd = [jnp.where(upper, rolled[i], tiles[i + 1]) for i in (0, 2)]
    ref[:, 0] = jnp.concatenate(even, axis=1).astype(BF16)
    ref[:, 1] = jnp.concatenate(odd, axis=1).astype(BF16)


def from_chunks(ref):
    even, odd = ref[:, 0].astype(F32), ref[:, 1].astype(F32)
    rows, width = even.shape[0] * 8, even.shape[2]
    upper = iota((1, 8, 1), 1) < HALF_TILE
    parts = []
    for i in (0, 1):
        e, o = even[:, 8 * i:8 * i + 8], odd[:, 8 * i:8 * i + 8]
        parts.append(jnp.where(upper, e, pltpu.roll(o, HALF_TILE, 1)).reshape(rows, width))
        parts.append(jnp.where(upper, pltpu.roll(e, HALF_TILE, 1), o).reshape(rows, width))
    return parts


def layer_kernel(
    dims, ids_ref, target_ref, table_ref, blocks_ref, across_ref, channel_ref, gain_ref, head_ref,
    out_ref, loss_ref,
    tall, x_send, x_recv, flipped, x_all, h_all, r_send, r_recv, s_send, s_recv,
    factors, gates, mix, spread, gather, padded, sums,
    buf_y, buf_w, buf_d, buf_l, own_y, own_w, own_l,
    x_sem, r_sem, s_sem, f_send, f_recv, g_send, g_recv, local_sem,
    send_y, recv_y, send_w, recv_w, send_d, recv_d, send_l, recv_l,
):
    n_d, n_c, seq_len = dims
    at = Place(n_d, n_c)
    feats, vocab = table_ref.shape
    block = blocks_ref.shape[1]
    half = block // 2
    width = channel_ref.shape[4]
    depth = channel_ref.shape[3]
    quarter = width // 4
    wide = gather.shape[0] // 4
    n_l = tall.shape[0] // feats
    n_z = at.z_size

    barrier = pltpu.get_barrier_semaphore()

    def greet(o, carry):
        pl.semaphore_signal(barrier, inc=1, device_id=(at.dp, at.ctx_at(o)), device_id_type=MESH)
        return carry

    lax.fori_loop(1, n_c, greet, 0)
    for o in range(1, n_d):
        pl.semaphore_signal(barrier, inc=1, device_id=at.d_peer(o), device_id_type=MESH)
    for step in (1, 2, n_z - 2, n_z - 1):
        pl.semaphore_signal(barrier, inc=1, device_id=at.z_at(step), device_id_type=MESH)

    def tall_pair(i, carry):
        start = pl.multiple_of(i * 2 * block, 2 * block)
        pair = table_ref[:, pl.ds(start, 2 * block)].astype(F32)
        tall[pl.ds(pl.multiple_of(i * 2 * feats, 2 * feats), 2 * feats), :] = jnp.concatenate(
            [pair[:, :block], pair[:, block:]], axis=0).astype(BF16)
        return carry

    full = vocab // (2 * block)
    lax.fori_loop(0, full, tall_pair, 0)
    if full * 2 < n_l:
        left = table_ref[:, full * 2 * block:].astype(F32)
        left = jnp.concatenate(
            [left, jnp.zeros((feats, 2 * block - left.shape[1]), F32)], axis=1)
        tall[full * 2 * feats:, :] = jnp.concatenate(
            [left[:, :block], left[:, block:]], axis=0).astype(BF16)

    pl.semaphore_wait(barrier, n_c - 1 + n_d - 1 + 4)

    def shard(m, dp):
        return factors.at[m, :, :, pl.ds(pl.multiple_of(dp * depth, depth), depth), :]

    steps = (1, n_z - 1, lax.rem(2 + at.core * (n_z - 4), n_z))
    sources = []
    for step in steps:
        sources.append(at.z_at(n_z - step)[0])
    pending = []
    for m in range(2):
        for j, step in enumerate(steps):
            copy = remote(channel_ref.at[m], shard(m, at.dp), f_send.at[m, j], f_recv.at[m, j],
                          at.z_at(step))
            copy.start()
            pending.append(copy)
    own_factors = []
    for m in range(2):
        copy = pltpu.make_async_copy(channel_ref.at[m], shard(m, at.dp), local_sem.at[m])
        copy.start()
        own_factors.append(copy)

    def lookup(i, carry):
        dest = at.ctx_at(n_c - 1 - i)
        ids = ids_ref[pl.ds(dest, 1), :]
        low, high = lax.rem(ids, block), ids // block
        hot = jnp.where(iota((block, block), 0) == low, 1.0, 0.0).astype(BF16)
        found = jnp.zeros((feats, block), F32)
        picked = dot(tall[...], hot)
        for l in range(n_l):
            found = jnp.where(high == l, picked[l * feats:(l + 1) * feats], found)
        x_send[dest] = jnp.concatenate([found[:, :half], found[:, half:]], axis=0).astype(BF16)

        @pl.when(i < n_c - 1)
        def _():
            remote(x_send.at[dest], x_recv.at[at.ctx], x_sem.at[0], x_sem.at[1],
                   (at.dp, dest)).start()

        @pl.when(i == n_c - 1)
        def _():
            pltpu.make_async_copy(x_send.at[dest], x_recv.at[at.ctx], x_sem.at[1]).start()

        return carry

    lax.fori_loop(0, n_c, lookup, 0)

    sibling = (at.dp + 1 - 2 * at.core, at.ctx)
    other = at.dp + 1 - 2 * at.core
    for m in range(2):
        own_factors[m].wait()
        for j, source in enumerate([at.dp] + sources):
            if j:
                remote(channel_ref.at[m], shard(m, source), f_send.at[m, j - 1],
                       f_recv.at[m, j - 1], sibling).wait_recv()
            copy = remote(shard(m, source), shard(m, source), g_send.at[m, j], g_recv.at[m, j],
                          sibling)
            copy.start()
            pending.append(copy)

    group = across_ref.shape[1]
    tall_one = jnp.where(iota((block, n_c), 0) // group == iota((block, n_c), 1), 1.0, 0.0)
    wide_one = jnp.where(iota((n_c, block), 1) // group == iota((n_c, block), 0), 1.0, 0.0)
    row_b, col_b = lax.rem(iota((block, block), 0), group), lax.rem(iota((block, block), 1), group)
    for m in range(2):
        total = jnp.zeros((block, block), F32)
        for b in range(group):
            piece = dot(dot(tall_one.astype(BF16), across_ref[m, b]).astype(BF16),
                        wide_one.astype(BF16))
            total = jnp.where((row_b == b) & (col_b == b), piece, total)
        mix[m] = total.astype(BF16)
    place, lane = iota((width, 4 * wide), 0), iota((width, 4 * wide), 1)
    inner = lax.rem(lane, wide)
    spread[...] = jnp.where(
        (place == (lane // wide) * quarter + inner) & (inner < quarter), 1.0, 0.0).astype(BF16)
    place, lane = iota((4 * wide, width), 0), iota((4 * wide, width), 1)
    inner = lax.rem(place, wide)
    gather[...] = jnp.where(
        (lane == inner * 4 + place // wide) & (inner < quarter), 1.0, 0.0).astype(BF16)

    def all_sent(buf, sem):
        if len(buf.shape) == 3:
            view = buf.at[pl.ds(0, n_c - 1)]
            pltpu.make_async_copy(view, view, sem).wait()
        else:
            view = buf.at[pl.ds(0, n_c // 2 - 1)]
            pltpu.make_async_copy(view, view, sem).wait()
            view = buf.at[0, 0]
            pltpu.make_async_copy(view, view, sem).wait()

    def send_all(send, recv, sems):
        def one(i, carry):
            dest = at.ctx_at(n_c - 1 - i)
            remote(send.at[dest // 2, lax.rem(dest, 2)],
                   recv.at[at.ctx // 2, lax.rem(at.ctx, 2)],
                   sems.at[0], sems.at[1], (at.dp, dest)).start()
            return carry

        lax.fori_loop(0, n_c - 1, one, 0)
        pltpu.make_async_copy(send.at[at.ctx // 2, lax.rem(at.ctx, 2)],
                              recv.at[at.ctx // 2, lax.rem(at.ctx, 2)], sems.at[1]).start()

    pltpu.make_async_copy(x_recv, x_recv, x_sem.at[1]).wait()

    def flip(i, carry):
        both = x_recv[i].astype(F32)
        start = pl.multiple_of(i * feats, feats)
        flipped[0, pl.ds(start, feats), :] = both[:feats]
        flipped[1, pl.ds(start, feats), :] = both[feats:]
        return carry

    lax.fori_loop(0, n_c, flip, 0)
    squares = []
    for i in range(2):
        square = jnp.zeros((half, 1), F32)
        for k in range(4):
            values = flipped[i, k * width:(k + 1) * width, :].T
            square = square + jnp.sum(values * values, axis=1, keepdims=True)
            x_all[k, i * half:(i + 1) * half, :] = values
        squares.append(square)
    scale = lax.rsqrt(jnp.concatenate(squares, axis=0) / (4 * width) + 1e-06)

    for m in range(2):
        parts = []
        for k in range(4):
            gain = gain_ref[m:m + 1, k * width:(k + 1) * width].astype(F32)
            h = (x_all[k] * scale * gain).astype(BF16)
            h_all[m, k] = h
            parts.append(dot(blocks_ref[m], h))
        to_chunks(parts, r_send.at[m])
        send_all(r_send.at[m], r_recv.at[m], r_sem.at[m])

    def gate(m):
        for j in range(4):
            source = (at.dp if j == 0 else sources[j - 1]) + 1 - 2 * at.core
            remote(shard(m, source), shard(m, source), g_send.at[m, j], g_recv.at[m, j],
                   sibling).wait_recv()
        for k in range(4):
            first = dot(h_all[m, k], factors[m, 0, k]).astype(BF16)
            first = dot(first, spread[...]).astype(BF16)
            for q in range(4):
                padded[q, :, k * wide:(k + 1) * wide] = first[:, q * wide:(q + 1) * wide]
        for q in range(4):
            second = dot(gather[...], factors[m, 1, q]).astype(BF16)
            z = dot(padded[q], second)
            gates[m, q] = 1.0 / (1.0 + jnp.exp(-z))

    gate(0)
    for m in range(2):
        pltpu.make_async_copy(r_recv.at[m], r_recv.at[m], r_sem.at[m, 1]).wait()
        parts = from_chunks(r_recv.at[m])
        to_chunks([dot(mix[m], part.astype(BF16)) for part in parts], s_send.at[m])
        send_all(s_send.at[m], s_recv.at[m], s_sem.at[m])
    gate(1)
    for m in range(2):
        pltpu.make_async_copy(s_recv.at[m], s_recv.at[m], s_sem.at[m, 1]).wait()
        parts = from_chunks(s_recv.at[m])
        for k in range(4):
            y = (x_all[k] + parts[k] * gates[m, k]).astype(BF16)
            if m == 0:
                out_ref[:, k * width:(k + 1) * width] = y
            sums[m * 4 + k:m * 4 + k + 1, :] = jnp.sum(y.astype(F32), axis=0, keepdims=True)

    pending += exchange(sums, buf_y, send_y, recv_y, at.y_peer, at.y, at.n_y)
    own_y[...] = total_of(buf_y, at.n_y)
    pending += exchange(own_y, buf_w, send_w, recv_w, at.w_peer, at.w, at.n_w)
    own_w[...] = total_of(buf_w, at.n_w) / seq_len
    pending += exchange(own_w, buf_d, send_d, recv_d, at.d_peer, at.dp, n_d)
    local = []
    for m in range(2):
        mine = (iota((8, 1), 0) == m * 4 + at.dp * 4 // n_d).astype(F32)
        model = (iota((8, 1), 0) // 4 == m).astype(F32)
        rows, norms = [], []
        for n in range(n_d):
            pooled = buf_d[n]
            rows.append(jnp.sum(pooled * mine, axis=0, keepdims=True))
            square = jnp.sum(pooled * pooled * model, axis=0, keepdims=True)
            norms.append(jnp.sum(square, axis=1, keepdims=True))
        norm = lax.rsqrt(jnp.concatenate(norms, axis=0) / (4 * width) + 1e-06)
        local.append(jnp.dot(jnp.concatenate(rows, axis=0) * norm, head_ref[m],
                             precision=lax.Precision.HIGHEST, preferred_element_type=F32))
    own_l[...] = jnp.concatenate(local, axis=1)
    pending += exchange(own_l, buf_l, send_l, recv_l, at.d_peer, at.dp, n_d)
    logits = total_of(buf_l, n_d)
    classes = logits.shape[1] // 2
    chosen = iota((n_d, classes), 1) == target_ref[...]
    losses = []
    for part in (logits[:, :classes], logits[:, classes:]):
        top = jnp.max(part, axis=1, keepdims=True)
        summed = jnp.log(jnp.sum(jnp.exp(part - top), axis=1, keepdims=True)) + top
        losses.append(summed - jnp.sum(jnp.where(chosen, part, 0.0), axis=1, keepdims=True))
    loss_ref[...] = jnp.broadcast_to(losses[0] - losses[1], loss_ref.shape)

    all_sent(x_send, x_sem.at[0])
    for m in range(2):
        all_sent(r_send.at[m], r_sem.at[m, 0])
        all_sent(s_send.at[m], s_sem.at[m, 0])
    for copy in pending:
        copy.wait_send()


def layer_call(ids, target, table, blocks, across, channel, gain, head, seq_len):
    n_d, n_c = lax.axis_size("dp"), lax.axis_size("ctx")
    n_w = 8 if n_c == 64 else 2
    n_y = n_c // n_w
    feats, vocab = table.shape
    block = blocks.shape[1]
    width, depth = channel.shape[4], channel.shape[3]
    wide = -(-(width // 4) // 128) * 128
    n_l = -(-vocab // (2 * block)) * 2
    classes = head.shape[2]
    dma = pltpu.SemaphoreType.DMA
    chunks = (2, n_c // 2, 2, 16, width)
    return pl.pallas_call(
        functools.partial(layer_kernel, (n_d, n_c, seq_len)),
        out_shape=(jax.ShapeDtypeStruct((block, 4 * width), BF16),
                   jax.ShapeDtypeStruct((n_d, 128), F32)),
        in_specs=[pl.BlockSpec(memory_space=pltpu.VMEM)] * 8,
        out_specs=(pl.BlockSpec(memory_space=pltpu.VMEM), pl.BlockSpec(memory_space=pltpu.VMEM)),
        scratch_shapes=[
            pltpu.VMEM((n_l * feats, block), BF16),
            pltpu.VMEM((n_c, 2 * feats, block // 2), BF16),
            pltpu.VMEM((n_c, 2 * feats, block // 2), BF16),
            pltpu.VMEM((2, n_c * feats, block // 2), F32),
            pltpu.VMEM((4, block, width), F32),
            pltpu.VMEM((2, 4, block, width), BF16),
            pltpu.VMEM(chunks, BF16), pltpu.VMEM(chunks, BF16),
            pltpu.VMEM(chunks, BF16), pltpu.VMEM(chunks, BF16),
            pltpu.VMEM((2, 2, 4, depth * n_d, width), BF16),
            pltpu.VMEM((2, 4, block, width), F32),
            pltpu.VMEM((2, block, block), BF16),
            pltpu.VMEM((width, 4 * wide), BF16), pltpu.VMEM((4 * wide, width), BF16),
            pltpu.VMEM((4, block, 4 * wide), BF16),
            pltpu.VMEM((8, width), F32),
            pltpu.VMEM((n_y, 8, width), F32), pltpu.VMEM((n_w, 8, width), F32),
            pltpu.VMEM((n_d, 8, width), F32), pltpu.VMEM((n_d, n_d, 2 * classes), F32),
            pltpu.VMEM((8, width), F32), pltpu.VMEM((8, width), F32),
            pltpu.VMEM((n_d, 2 * classes), F32),
            dma((2,)), dma((2, 2)), dma((2, 2)),
            dma((2, 3)), dma((2, 3)), dma((2, 4)), dma((2, 4)), dma((2,)),
            dma((n_y,)), dma((n_y,)), dma((n_w,)), dma((n_w,)),
            dma((n_d,)), dma((n_d,)), dma((n_d,)), dma((n_d,)),
        ],
        compiler_params=pltpu.CompilerParams(
            collective_id=1, has_side_effects=True, vmem_limit_bytes=56 * 1024 * 1024),
        name="layer",
    )(ids, target, table, blocks, across, channel, gain, head)


def body(
    token_ids,
    target_ids,
    candidates,
    embed_table,
    online_blocks,
    online_across,
    online_channel,
    online_gain,
    online_head,
    ref_blocks,
    ref_across,
    ref_channel,
    ref_gain,
    ref_head,
):
    n_d, n_c = lax.axis_size("dp"), lax.axis_size("ctx")
    seq_len = token_ids.shape[1]
    heads = jnp.stack([online_head, ref_head]).astype(F32)
    part = heads.shape[1]
    reps = n_d // 4
    slot = lax.rem(lax.axis_index("dp"), reps)
    rows = jnp.arange(part * reps, dtype=jnp.int32) // part
    head = jnp.where((rows == slot)[None, :, None], jnp.concatenate([heads] * reps, axis=1), 0.0)
    out, loss = layer_call(
        token_ids.reshape(n_c, seq_len // n_c),
        target_ids.reshape(n_d, 1),
        embed_table,
        jnp.concatenate([online_blocks, ref_blocks]),
        jnp.stack([online_across, ref_across]),
        jnp.stack([online_channel, ref_channel]),
        jnp.stack([online_gain, ref_gain]),
        head,
        seq_len,
    )
    scores = loss[:, 0]
    pick_mask = (candidates[:, None] == jnp.arange(n_d, dtype=jnp.int32)[None]).astype(F32)
    picked = jnp.sum(pick_mask * scores[None], axis=1)
    return (out, scores, picked)


def solution(mesh):
    in_specs = (
        P("dp", None),
        P(),
        P(),
        P("ctx", None),
        P("ctx", None, None),
        P("ctx", None, None),
        P(None, None, "dp", None),
        P(),
        P("dp", None),
        P("ctx", None, None),
        P("ctx", None, None),
        P(None, None, "dp", None),
        P(),
        P("dp", None),
    )
    out_specs = (P(("dp", "ctx"), None), P(), P())
    return jax.shard_map(body, mesh=mesh, in_specs=in_specs, out_specs=out_specs, check_vma=False)
```

```python
import functools
import jax
import jax.numpy as jnp
from jax import lax
from jax.experimental import pallas as pl
from jax.experimental.pallas import tpu as pltpu
from jax.sharding import PartitionSpec as P

MESH = pl.DeviceIdType.MESH
F32 = jnp.float32
BF16 = jnp.bfloat16
HALF_TILE = 4


def dot(a, b):
    return jnp.dot(a, b, preferred_element_type=F32)


def iota(shape, axis):
    return lax.broadcasted_iota(jnp.int32, shape, axis)


class Place:
    def __init__(self, n_d, n_c):
        self.n_d, self.n_c = n_d, n_c
        self.n_x = 4 if n_c == 64 else n_c // 2
        self.n_y = n_c // (2 * self.n_x)
        self.n_w = 2 * self.n_x
        self.z_lo_size = n_d // 2
        self.z_size = 2 * self.z_lo_size
        self.dp, self.ctx = lax.axis_index("dp"), lax.axis_index("ctx")
        self.y, self.w = self.ctx // self.n_w, lax.rem(self.ctx, self.n_w)
        self.z_hi, self.x = self.w // self.n_x, lax.rem(self.w, self.n_x)
        self.z_lo, self.core = self.dp // 2, lax.rem(self.dp, 2)
        self.z = self.z_hi * self.z_lo_size + self.z_lo

    def ctx_at(self, o):
        step_y = lax.rem(lax.rem(o, self.n_y) * 3, self.n_y)
        rest = o // self.n_y
        step_z, step_x = lax.rem(rest, 2), rest // 2
        y = lax.rem(self.y + step_y, self.n_y)
        z_hi = lax.rem(self.z_hi + step_z, 2)
        x = lax.rem(self.x + step_x, self.n_x)
        return y * self.n_w + z_hi * self.n_x + x

    def z_at(self, step):
        z = lax.rem(self.z + step, self.z_size)
        dp = lax.rem(z, self.z_lo_size) * 2 + self.core
        ctx = self.y * self.n_w + (z // self.z_lo_size) * self.n_x + self.x
        return dp, ctx

    def x_peer(self, o):
        x = lax.rem(self.x + o, self.n_x)
        return (self.dp, self.y * self.n_w + self.z_hi * self.n_x + x)

    def y_peer(self, o):
        return (self.dp, lax.rem(self.y + o, self.n_y) * self.n_w + self.w)

    def w_peer(self, o):
        return (self.dp, self.y * self.n_w + lax.rem(self.w + o, self.n_w))

    def d_peer(self, o):
        return (lax.rem(self.dp + o, self.n_d), self.ctx)


def remote(src, dst, send, recv, device):
    return pltpu.make_async_remote_copy(
        src_ref=src, dst_ref=dst, send_sem=send, recv_sem=recv,
        device_id=device, device_id_type=MESH)


def spread_out(own, buf, send, recv, peer, me, count):
    copies = []
    for o in range(1, count):
        copy = remote(own, buf.at[me], send.at[o], recv.at[me], peer(o))
        copy.start()
        copies.append(copy)
    buf[me] = own[...]
    return copies


def gathered(own, buf, send, recv, peer, me, count):
    for o in range(1, count):
        slot = lax.rem(me + o, count)
        remote(own, buf.at[slot], send.at[o], recv.at[slot], peer(o)).wait_recv()


def total_of(buf, count):
    total = buf[0]
    for j in range(1, count):
        total = total + buf[j]
    return total


def to_chunks(parts, ref):
    rows, width = parts[0].shape
    tiles = [p.reshape(rows // 8, 8, width) for p in parts]
    rolled = [pltpu.roll(t, HALF_TILE, 1) for t in tiles]
    upper = iota((1, 8, 1), 1) < HALF_TILE
    even = [jnp.where(upper, tiles[i], rolled[i + 1]) for i in (0, 2)]
    odd = [jnp.where(upper, rolled[i], tiles[i + 1]) for i in (0, 2)]
    ref[:, 0] = jnp.concatenate(even, axis=1).astype(BF16)
    ref[:, 1] = jnp.concatenate(odd, axis=1).astype(BF16)


def from_chunks(ref):
    even, odd = ref[:, 0].astype(F32), ref[:, 1].astype(F32)
    rows, width = even.shape[0] * 8, even.shape[2]
    upper = iota((1, 8, 1), 1) < HALF_TILE
    parts = []
    for i in (0, 1):
        e, o = even[:, 8 * i:8 * i + 8], odd[:, 8 * i:8 * i + 8]
        parts.append(jnp.where(upper, e, pltpu.roll(o, HALF_TILE, 1)).reshape(rows, width))
        parts.append(jnp.where(upper, pltpu.roll(e, HALF_TILE, 1), o).reshape(rows, width))
    return parts


def layer_kernel(
    dims, ids_ref, target_ref, candidate_ref, table_ref,
    online_blocks, online_across, online_channel, online_gain, online_head,
    frozen_blocks, frozen_across, frozen_channel, frozen_gain, frozen_head,
    out_ref, score_ref,
    tall, xa_send, xa_recv, xb_send, xb_recv, flipped, x_all, r_send, r_recv, y_send, y_recv,
    factors, gates, mix, spread, gather, padded, sums,
    buf_y, buf_w, buf_d, buf_l, own_y, own_w, own_l,
    xa_sem, xb_sem, r_sem, y_sem, f_send, f_recv, e_send, e_recv, g_send, g_recv, local_sem,
    send_y, recv_y, send_w, recv_w, send_d, recv_d, send_l, recv_l,
):
    n_d, n_c, seq_len = dims
    at = Place(n_d, n_c)
    blocks_refs = (online_blocks, frozen_blocks)
    across_refs = (online_across, frozen_across)
    channel_refs = (online_channel, frozen_channel)
    gain_refs = (online_gain, frozen_gain)
    head_refs = (online_head, frozen_head)
    feats, vocab = table_ref.shape
    block = online_blocks.shape[1]
    half = block // 2
    depth, width = online_channel.shape[2:]
    quarter = width // 4
    wide = gather.shape[0] // 4
    n_l = tall.shape[0] // feats
    n_z = at.z_size
    group = online_across.shape[0]

    barrier = pltpu.get_barrier_semaphore()

    def greet(o, carry):
        pl.semaphore_signal(barrier, inc=1, device_id=(at.dp, at.ctx_at(o)), device_id_type=MESH)
        return carry

    lax.fori_loop(1, n_c, greet, 0)
    for o in range(1, n_d):
        pl.semaphore_signal(barrier, inc=1, device_id=at.d_peer(o), device_id_type=MESH)
    for step in (1, 2, n_z - 2, n_z - 1):
        pl.semaphore_signal(barrier, inc=1, device_id=at.z_at(step), device_id_type=MESH)

    def tall_pair(i, carry):
        start = pl.multiple_of(i * 2 * block, 2 * block)
        pair = table_ref[:, pl.ds(start, 2 * block)].astype(F32)
        tall[pl.ds(pl.multiple_of(i * 2 * feats, 2 * feats), 2 * feats), :] = jnp.concatenate(
            [pair[:, :block], pair[:, block:]], axis=0).astype(BF16)
        return carry

    full = vocab // (2 * block)
    lax.fori_loop(0, full, tall_pair, 0)
    if full * 2 < n_l:
        left = table_ref[:, full * 2 * block:].astype(F32)
        left = jnp.concatenate(
            [left, jnp.zeros((feats, 2 * block - left.shape[1]), F32)], axis=1)
        tall[full * 2 * feats:, :] = jnp.concatenate(
            [left[:, :block], left[:, block:]], axis=0).astype(BF16)

    pl.semaphore_wait(barrier, n_c - 1 + n_d - 1 + 4)

    n_k = 4 // at.n_x

    def shard(m, dp, x=None):
        rows = pl.ds(pl.multiple_of(dp * depth, depth), depth)
        if x is None:
            return factors.at[m, :, :, rows, :]
        return factors.at[m, :, pl.ds(x * n_k, n_k), rows, :]

    steps = (1, n_z - 1, lax.rem(2 + at.core * (n_z - 4), n_z))
    sources = [at.z_at(n_z - step)[0] for step in steps]
    pending = []
    for m in range(2):
        for j, step in enumerate(steps):
            copy = remote(channel_refs[m].at[:, pl.ds(at.x * n_k, n_k)], shard(m, at.dp, at.x),
                          f_send.at[m, j], f_recv.at[m, j], at.z_at(step))
            copy.start()
            pending.append(copy)
    own_factors = []
    for m in range(2):
        copy = pltpu.make_async_copy(channel_refs[m], shard(m, at.dp), local_sem.at[m])
        copy.start()
        own_factors.append(copy)

    def send_found(low, high, i, dest, send, recv, sems):
        hot = jnp.where(iota((block, block), 0).astype(F32) == low, 1.0, 0.0).astype(BF16)
        found = jnp.zeros((feats, block), F32)
        picked = dot(tall[...], hot)
        for l in range(n_l):
            found = jnp.where(high == float(l), picked[l * feats:(l + 1) * feats], found)
        send[dest] = jnp.concatenate([found[:, :half], found[:, half:]], axis=0).astype(BF16)

        @pl.when(i < n_c - 1)
        def _():
            remote(send.at[dest], recv.at[at.ctx], sems.at[0], sems.at[1], (at.dp, dest)).start()

        @pl.when(i == n_c - 1)
        def _():
            pltpu.make_async_copy(send.at[dest], recv.at[at.ctx], sems.at[1]).start()

    def lookup_own(i, carry):
        dest = at.ctx_at(n_c - 1 - i)
        ids = ids_ref[pl.ds(dest, 1), :]
        low, high = lax.rem(ids, block).astype(F32), (ids // block).astype(F32)
        send_found(low, high, i, dest, xa_send, xa_recv, xa_sem)
        return carry

    def lookup_across(i, carry):
        dest = at.ctx_at(n_c - 1 - i)
        ids = ids_ref[...]
        both = jnp.concatenate([lax.rem(ids, block), ids // block], axis=0)
        offset = lax.rem(iota((block, block), 1), group) + dest * group
        pick = jnp.where(iota((block, block), 0) == offset, 1.0, 0.0).astype(BF16)
        both = dot(both.astype(F32).astype(BF16), pick)
        mine = iota((n_c, block), 1) // group == iota((n_c, block), 0)
        low = jnp.sum(jnp.where(mine, both[:n_c], 0.0), axis=0, keepdims=True)
        high = jnp.sum(jnp.where(mine, both[n_c:], 0.0), axis=0, keepdims=True)
        send_found(low, high, i, dest, xb_send, xb_recv, xb_sem)
        return carry

    def unpack(recv, sems):
        pltpu.make_async_copy(recv, recv, sems.at[1]).wait()

        def flip(i, carry):
            both = recv[i].astype(F32)
            start = pl.multiple_of(i * feats, feats)
            flipped[0, pl.ds(start, feats), :] = both[:feats]
            flipped[1, pl.ds(start, feats), :] = both[feats:]
            return carry

        lax.fori_loop(0, n_c, flip, 0)
        squares = []
        for i in range(2):
            square = jnp.zeros((half, 1), F32)
            for k in range(4):
                values = flipped[i, k * width:(k + 1) * width, :].T
                square = square + jnp.sum(values * values, axis=1, keepdims=True)
                x_all[k, i * half:(i + 1) * half, :] = values
            squares.append(square)
        return lax.rsqrt(jnp.concatenate(squares, axis=0) / (4 * width) + 1e-06)

    def normed(m, k, scale):
        gain = gain_refs[m][:, k * width:(k + 1) * width].astype(F32)
        return (x_all[k] * scale * gain).astype(BF16)

    def send_part(send, recv, sems, first, last):
        def one(i, carry):
            dest = at.ctx_at(n_c - 1 - i)
            remote(send.at[dest // 2, lax.rem(dest, 2)],
                   recv.at[at.ctx // 2, lax.rem(at.ctx, 2)],
                   sems.at[0], sems.at[1], (at.dp, dest)).start()
            return carry

        lax.fori_loop(first, last, one, 0)

    def keep_own(send, recv, sems):
        pltpu.make_async_copy(send.at[at.ctx // 2, lax.rem(at.ctx, 2)],
                              recv.at[at.ctx // 2, lax.rem(at.ctx, 2)], sems.at[1]).start()

    def within(m, scale):
        to_chunks([dot(blocks_refs[m][0], normed(m, k, scale)) for k in range(4)], r_send.at[m])
        send_part(r_send.at[m], r_recv.at[m], r_sem.at[m], 0, n_c - 1)
        keep_own(r_send.at[m], r_recv.at[m], r_sem.at[m])

    lax.fori_loop(0, n_c, lookup_own, 0)

    for m in range(2):
        for j, source in enumerate(sources):
            remote(shard(m, source, at.x), shard(m, source, at.x), f_send.at[m, j],
                   f_recv.at[m, j], at.z_at(steps[j])).wait_recv()
            for o in range(1, at.n_x):
                copy = remote(shard(m, source, at.x), shard(m, source, at.x),
                              e_send.at[m, j, o - 1], e_recv.at[m, j, o - 1], at.x_peer(o))
                copy.start()
                pending.append(copy)

    scale = unpack(xa_recv, xa_sem)
    within(0, scale)
    lax.fori_loop(0, n_c, lookup_across, 0)
    within(1, scale)

    other = at.dp + 1 - 2 * at.core
    sibling = (other, at.ctx)
    for m in range(2):
        own_factors[m].wait()
        for j, source in enumerate([at.dp] + sources):
            if j:
                for o in range(1, at.n_x):
                    part = shard(m, source, lax.rem(at.x + at.n_x - o, at.n_x))
                    remote(part, part, e_send.at[m, j - 1, o - 1], e_recv.at[m, j - 1, o - 1],
                           at.x_peer(o)).wait_recv()
            copy = remote(shard(m, source), shard(m, source), g_send.at[m, j], g_recv.at[m, j],
                          sibling)
            copy.start()
            pending.append(copy)

    tall_one = jnp.where(iota((block, n_c), 0) // group == iota((block, n_c), 1), 1.0, 0.0)
    wide_one = jnp.where(iota((n_c, block), 1) // group == iota((n_c, block), 0), 1.0, 0.0)
    row_b, col_b = lax.rem(iota((block, block), 0), group), lax.rem(iota((block, block), 1), group)
    for m in range(2):
        total = jnp.zeros((block, block), F32)
        for b in range(group):
            piece = dot(dot(tall_one.astype(BF16), across_refs[m][b]).astype(BF16),
                        wide_one.astype(BF16))
            total = jnp.where((row_b == b) & (col_b == b), piece, total)
        mix[m] = total.astype(BF16)
    place, lane = iota((width, 4 * wide), 0), iota((width, 4 * wide), 1)
    inner = lax.rem(lane, wide)
    spread[...] = jnp.where(
        (place == (lane // wide) * quarter + inner) & (inner < quarter), 1.0, 0.0).astype(BF16)
    place, lane = iota((4 * wide, width), 0), iota((4 * wide, width), 1)
    inner = lax.rem(place, wide)
    gather[...] = jnp.where(
        (lane == inner * 4 + place // wide) & (inner < quarter), 1.0, 0.0).astype(BF16)

    scale = unpack(xb_recv, xb_sem)
    for m in range(2):
        for j in range(4):
            source = (at.dp if j == 0 else sources[j - 1]) + 1 - 2 * at.core
            remote(shard(m, source), shard(m, source), g_send.at[m, j], g_recv.at[m, j],
                   sibling).wait_recv()
        for k in range(4):
            first = dot(normed(m, k, scale), factors[m, 0, k]).astype(BF16)
            first = dot(first, spread[...]).astype(BF16)
            for q in range(4):
                padded[q, :, k * wide:(k + 1) * wide] = first[:, q * wide:(q + 1) * wide]
        for q in range(4):
            second = dot(gather[...], factors[m, 1, q]).astype(BF16)
            z = dot(padded[q], second)
            gates[m, q] = 1.0 / (1.0 + jnp.exp(-z))

    for m in range(2):
        pltpu.make_async_copy(r_recv.at[m], r_recv.at[m], r_sem.at[m, 1]).wait()
        parts = from_chunks(r_recv.at[m])
        outputs = []
        for k in range(4):
            mixed = dot(mix[m], parts[k].astype(BF16)).astype(BF16).astype(F32)
            y = (x_all[k] + mixed * gates[m, k]).astype(BF16).astype(F32)
            sums[m * 4 + k:m * 4 + k + 1, :] = jnp.sum(y, axis=0, keepdims=True)
            outputs.append(y)
        if m == 0:
            to_chunks(outputs, y_send)
            keep_own(y_send, y_recv, y_sem)
            send_part(y_send, y_recv, y_sem, 0, n_c // 8)

    stage = (sums, buf_y, send_y, recv_y, at.y_peer, at.y, at.n_y)
    pending += spread_out(*stage)
    send_part(y_send, y_recv, y_sem, n_c // 8, n_c // 8 * 3)
    gathered(*stage)
    own_y[...] = total_of(buf_y, at.n_y)
    stage = (own_y, buf_w, send_w, recv_w, at.w_peer, at.w, at.n_w)
    pending += spread_out(*stage)
    send_part(y_send, y_recv, y_sem, n_c // 8 * 3, n_c // 8 * 5)
    gathered(*stage)
    own_w[...] = total_of(buf_w, at.n_w) / seq_len
    stage = (own_w, buf_d, send_d, recv_d, at.d_peer, at.dp, n_d)
    pending += spread_out(*stage)
    send_part(y_send, y_recv, y_sem, n_c // 8 * 5, n_c // 8 * 7)
    gathered(*stage)
    local = []
    reps = n_d // 4
    for m in range(2):
        mine = (iota((8, 1), 0) == m * 4 + at.dp // reps).astype(F32)
        model = (iota((8, 1), 0) // 4 == m).astype(F32)
        rows, norms = [], []
        for n in range(n_d):
            pooled = buf_d[n]
            rows.append(jnp.sum(pooled * mine, axis=0, keepdims=True))
            square = jnp.sum(pooled * pooled * model, axis=0, keepdims=True)
            norms.append(jnp.sum(square, axis=1, keepdims=True))
        norm = lax.rsqrt(jnp.concatenate(norms, axis=0) / (4 * width) + 1e-06)
        head = head_refs[m][...].astype(F32)
        slot = iota((width, 1), 0) // (width // reps)
        head = jnp.where(slot == lax.rem(at.dp, reps), jnp.concatenate([head] * reps, axis=0), 0.0)
        local.append(jnp.dot(jnp.concatenate(rows, axis=0) * norm, head,
                             precision=lax.Precision.HIGHEST, preferred_element_type=F32))
    own_l[...] = jnp.concatenate(local, axis=1)
    stage = (own_l, buf_l, send_l, recv_l, at.d_peer, at.dp, n_d)
    pending += spread_out(*stage)
    send_part(y_send, y_recv, y_sem, n_c // 8 * 7, n_c - 1)
    gathered(*stage)
    logits = total_of(buf_l, n_d)
    classes = logits.shape[1] // 2
    row = iota((n_d, 1), 0)
    target = jnp.zeros((n_d, 1), jnp.int32)
    for n in range(n_d):
        target = jnp.where(row == n, target_ref[n], target)
    chosen = iota((n_d, classes), 1) == target
    losses = []
    for part in (logits[:, :classes], logits[:, classes:]):
        top = jnp.max(part, axis=1, keepdims=True)
        summed = jnp.log(jnp.sum(jnp.exp(part - top), axis=1, keepdims=True)) + top
        losses.append(summed - jnp.sum(jnp.where(chosen, part, 0.0), axis=1, keepdims=True))
    scores = losses[0] - losses[1]
    lane = iota((1, 128), 1)
    wanted = jnp.where(lane < n_d, lane, -1)
    for k in range(candidate_ref.shape[0]):
        wanted = jnp.where(lane == n_d + k, candidate_ref[k], wanted)
    score_ref[...] = jnp.sum(jnp.where(row == wanted, scores, 0.0), axis=0, keepdims=True)

    pltpu.make_async_copy(y_recv, y_recv, y_sem.at[1]).wait()
    parts = from_chunks(y_recv)
    for k in range(4):
        out_ref[:, k * width:(k + 1) * width] = parts[k].astype(BF16)

    def sent(view, sem):
        pltpu.make_async_copy(view, view, sem).wait()

    sent(xa_send.at[pl.ds(0, n_c - 1)], xa_sem.at[0])
    sent(xb_send.at[pl.ds(0, n_c - 1)], xb_sem.at[0])
    for buf, sem in ((r_send.at[0], r_sem.at[0, 0]), (r_send.at[1], r_sem.at[1, 0]),
                     (y_send, y_sem.at[0])):
        sent(buf.at[pl.ds(0, n_c // 2 - 1)], sem)
        sent(buf.at[0, 0], sem)
    for copy in pending:
        copy.wait_send()


def layer_call(ids, target, candidates, table, online, frozen, seq_len):
    n_d, n_c = lax.axis_size("dp"), lax.axis_size("ctx")
    n_x = 4 if n_c == 64 else n_c // 2
    n_w = 2 * n_x
    n_y = n_c // n_w
    feats, vocab = table.shape
    block = online[0].shape[1]
    depth, width = online[2].shape[2:]
    wide = -(-(width // 4) // 128) * 128
    n_l = -(-vocab // (2 * block)) * 2
    classes = online[4].shape[1]
    dma = pltpu.SemaphoreType.DMA
    found = (n_c, 2 * feats, block // 2)
    chunks = (n_c // 2, 2, 16, width)
    vmem, smem = pl.BlockSpec(memory_space=pltpu.VMEM), pl.BlockSpec(memory_space=pltpu.SMEM)
    return pl.pallas_call(
        functools.partial(layer_kernel, (n_d, n_c, seq_len)),
        out_shape=(jax.ShapeDtypeStruct((block, 4 * width), BF16),
                   jax.ShapeDtypeStruct((1, 128), F32)),
        in_specs=[vmem, smem, smem] + [vmem] * 11,
        out_specs=(vmem, vmem),
        scratch_shapes=[
            pltpu.VMEM((n_l * feats, block), BF16),
            pltpu.VMEM(found, BF16), pltpu.VMEM(found, BF16),
            pltpu.VMEM(found, BF16), pltpu.VMEM(found, BF16),
            pltpu.VMEM((2, n_c * feats, block // 2), F32),
            pltpu.VMEM((4, block, width), F32),
            pltpu.VMEM((2,) + chunks, BF16), pltpu.VMEM((2,) + chunks, BF16),
            pltpu.VMEM(chunks, BF16), pltpu.VMEM(chunks, BF16),
            pltpu.VMEM((2, 2, 4, depth * n_d, width), BF16),
            pltpu.VMEM((2, 4, block, width), F32),
            pltpu.VMEM((2, block, block), BF16),
            pltpu.VMEM((width, 4 * wide), BF16), pltpu.VMEM((4 * wide, width), BF16),
            pltpu.VMEM((4, block, 4 * wide), BF16),
            pltpu.VMEM((8, width), F32),
            pltpu.VMEM((n_y, 8, width), F32), pltpu.VMEM((n_w, 8, width), F32),
            pltpu.VMEM((n_d, 8, width), F32), pltpu.VMEM((n_d, n_d, 2 * classes), F32),
            pltpu.VMEM((8, width), F32), pltpu.VMEM((8, width), F32),
            pltpu.VMEM((n_d, 2 * classes), F32),
            dma((2,)), dma((2,)), dma((2, 2)), dma((2,)),
            dma((2, 3)), dma((2, 3)), dma((2, 3, max(n_x - 1, 1))), dma((2, 3, max(n_x - 1, 1))),
            dma((2, 4)), dma((2, 4)), dma((2,)),
            dma((n_y,)), dma((n_y,)), dma((n_w,)), dma((n_w,)),
            dma((n_d,)), dma((n_d,)), dma((n_d,)), dma((n_d,)),
        ],
        compiler_params=pltpu.CompilerParams(
            collective_id=1, has_side_effects=True, vmem_limit_bytes=56 * 1024 * 1024),
        name="layer",
    )(ids, target, candidates, table, *online, *frozen)


def body(
    token_ids,
    target_ids,
    candidates,
    embed_table,
    online_blocks,
    online_across,
    online_channel,
    online_gain,
    online_head,
    ref_blocks,
    ref_across,
    ref_channel,
    ref_gain,
    ref_head,
):
    n_d, n_c = lax.axis_size("dp"), lax.axis_size("ctx")
    seq_len = token_ids.shape[1]
    out, scores = layer_call(
        token_ids.reshape(n_c, seq_len // n_c),
        target_ids,
        candidates,
        embed_table,
        (online_blocks, online_across, online_channel, online_gain[None], online_head),
        (ref_blocks, ref_across, ref_channel, ref_gain[None], ref_head),
        seq_len,
    )
    return (out, scores[0, :n_d], scores[0, n_d:n_d + candidates.shape[0]])


def solution(mesh):
    in_specs = (
        P("dp", None),
        P(),
        P(),
        P("ctx", None),
        P("ctx", None, None),
        P("ctx", None, None),
        P(None, None, "dp", None),
        P(),
        P("dp", None),
        P("ctx", None, None),
        P("ctx", None, None),
        P(None, None, "dp", None),
        P(),
        P("dp", None),
    )
    out_specs = (P(("dp", "ctx"), None), P(), P())
    return jax.shard_map(body, mesh=mesh, in_specs=in_specs, out_specs=out_specs, check_vma=False)
```

```python
import functools
import jax
import jax.numpy as jnp
from jax import lax
from jax.experimental import pallas as pl
from jax.experimental.pallas import tpu as pltpu
from jax.sharding import PartitionSpec as P

MESH = pl.DeviceIdType.MESH
F32 = jnp.float32
BF16 = jnp.bfloat16
HALF_TILE = 4


def dot(a, b):
    return jnp.dot(a, b, preferred_element_type=F32)


def iota(shape, axis):
    return lax.broadcasted_iota(jnp.int32, shape, axis)


class Place:
    def __init__(self, n_d, n_c):
        self.n_d, self.n_c = n_d, n_c
        self.n_x = 4 if n_c == 64 else n_c // 2
        self.n_y = n_c // (2 * self.n_x)
        self.n_w = 2 * self.n_x
        self.z_lo_size = n_d // 2
        self.z_size = 2 * self.z_lo_size
        self.dp, self.ctx = lax.axis_index("dp"), lax.axis_index("ctx")
        self.y, self.w = self.ctx // self.n_w, lax.rem(self.ctx, self.n_w)
        self.z_hi, self.x = self.w // self.n_x, lax.rem(self.w, self.n_x)
        self.z_lo, self.core = self.dp // 2, lax.rem(self.dp, 2)
        self.z = self.z_hi * self.z_lo_size + self.z_lo

    def ctx_at(self, o):
        step_y = lax.rem(lax.rem(o, self.n_y) * 3, self.n_y)
        rest = o // self.n_y
        step_z, step_x = lax.rem(rest, 2), rest // 2
        y = lax.rem(self.y + step_y, self.n_y)
        z_hi = lax.rem(self.z_hi + step_z, 2)
        x = lax.rem(self.x + step_x, self.n_x)
        return y * self.n_w + z_hi * self.n_x + x

    def z_at(self, step):
        z = lax.rem(self.z + step, self.z_size)
        dp = lax.rem(z, self.z_lo_size) * 2 + self.core
        ctx = self.y * self.n_w + (z // self.z_lo_size) * self.n_x + self.x
        return dp, ctx

    def x_peer(self, o):
        x = lax.rem(self.x + o, self.n_x)
        return (self.dp, self.y * self.n_w + self.z_hi * self.n_x + x)

    def y_peer(self, o):
        return (self.dp, lax.rem(self.y + o, self.n_y) * self.n_w + self.w)

    def w_peer(self, o):
        return (self.dp, self.y * self.n_w + lax.rem(self.w + o, self.n_w))

    def d_peer(self, o):
        return (lax.rem(self.dp + o, self.n_d), self.ctx)


def remote(src, dst, send, recv, device):
    return pltpu.make_async_remote_copy(
        src_ref=src, dst_ref=dst, send_sem=send, recv_sem=recv,
        device_id=device, device_id_type=MESH)


def spread_out(own, buf, send, recv, peer, me, count):
    copies = []
    for o in range(1, count):
        copy = remote(own, buf.at[me], send.at[o], recv.at[me], peer(o))
        copy.start()
        copies.append(copy)
    buf[me] = own[...]
    return copies


def gathered(own, buf, send, recv, peer, me, count):
    for o in range(1, count):
        slot = lax.rem(me + o, count)
        remote(own, buf.at[slot], send.at[o], recv.at[slot], peer(o)).wait_recv()


def total_of(buf, count):
    total = buf[0]
    for j in range(1, count):
        total = total + buf[j]
    return total


def to_chunks(parts, ref):
    rows, width = parts[0].shape
    tiles = [p.reshape(rows // 8, 8, width) for p in parts]
    rolled = [pltpu.roll(t, HALF_TILE, 1) for t in tiles]
    upper = iota((1, 8, 1), 1) < HALF_TILE
    even = [jnp.where(upper, tiles[i], rolled[i + 1]) for i in (0, 2)]
    odd = [jnp.where(upper, rolled[i], tiles[i + 1]) for i in (0, 2)]
    ref[:, 0] = jnp.concatenate(even, axis=1).astype(BF16)
    ref[:, 1] = jnp.concatenate(odd, axis=1).astype(BF16)


def from_chunks(ref):
    even, odd = ref[:, 0].astype(F32), ref[:, 1].astype(F32)
    rows, width = even.shape[0] * 8, even.shape[2]
    upper = iota((1, 8, 1), 1) < HALF_TILE
    parts = []
    for i in (0, 1):
        e, o = even[:, 8 * i:8 * i + 8], odd[:, 8 * i:8 * i + 8]
        parts.append(jnp.where(upper, e, pltpu.roll(o, HALF_TILE, 1)).reshape(rows, width))
        parts.append(jnp.where(upper, pltpu.roll(e, HALF_TILE, 1), o).reshape(rows, width))
    return parts


def layer_kernel(
    dims, ids_ref, target_ref, candidate_ref, table_ref,
    online_blocks, online_across, online_channel, online_gain, online_head,
    frozen_blocks, frozen_across, frozen_channel, frozen_gain, frozen_head,
    out_ref, score_ref, picked_ref,
    tall, xa_send, xa_recv, xb_send, xb_recv, flipped, x_all, r_send, r_recv, y_send, y_recv,
    factors, gates, mix, spread, gather, padded, sums,
    buf_y, buf_w, buf_d, buf_l, own_y, own_w, own_l,
    xa_sem, xb_sem, r_sem, y_sem, f_send, f_recv, e_send, e_recv, g_send, g_recv, local_sem,
    send_y, recv_y, send_w, recv_w, send_d, recv_d, send_l, recv_l,
):
    n_d, n_c, seq_len = dims
    at = Place(n_d, n_c)
    blocks_refs = (online_blocks, frozen_blocks)
    across_refs = (online_across, frozen_across)
    channel_refs = (online_channel, frozen_channel)
    gain_refs = (online_gain, frozen_gain)
    head_refs = (online_head, frozen_head)
    feats, vocab = table_ref.shape
    block = online_blocks.shape[1]
    half = block // 2
    depth, width = online_channel.shape[2:]
    quarter = width // 4
    wide = gather.shape[0] // 4
    n_l = tall.shape[0] // feats
    n_z = at.z_size
    group = online_across.shape[0]

    barrier = pltpu.get_barrier_semaphore()

    def greet(o, carry):
        pl.semaphore_signal(barrier, inc=1, device_id=(at.dp, at.ctx_at(o)), device_id_type=MESH)
        return carry

    lax.fori_loop(1, n_c, greet, 0)
    for o in range(1, n_d):
        pl.semaphore_signal(barrier, inc=1, device_id=at.d_peer(o), device_id_type=MESH)
    for step in (1, 2, n_z - 2, n_z - 1):
        pl.semaphore_signal(barrier, inc=1, device_id=at.z_at(step), device_id_type=MESH)

    def tall_pair(i, carry):
        start = pl.multiple_of(i * 2 * block, 2 * block)
        pair = table_ref[:, pl.ds(start, 2 * block)].astype(F32)
        tall[pl.ds(pl.multiple_of(i * 2 * feats, 2 * feats), 2 * feats), :] = jnp.concatenate(
            [pair[:, :block], pair[:, block:]], axis=0).astype(BF16)
        return carry

    full = vocab // (2 * block)
    lax.fori_loop(0, full, tall_pair, 0)
    if full * 2 < n_l:
        left = table_ref[:, full * 2 * block:].astype(F32)
        left = jnp.concatenate(
            [left, jnp.zeros((feats, 2 * block - left.shape[1]), F32)], axis=1)
        tall[full * 2 * feats:, :] = jnp.concatenate(
            [left[:, :block], left[:, block:]], axis=0).astype(BF16)

    pl.semaphore_wait(barrier, n_c - 1 + n_d - 1 + 4)

    n_k = 4 // at.n_x

    def shard(m, dp, x=None):
        rows = pl.ds(pl.multiple_of(dp * depth, depth), depth)
        if x is None:
            return factors.at[m, :, :, rows, :]
        return factors.at[m, :, pl.ds(x * n_k, n_k), rows, :]

    steps = (1, n_z - 1, lax.rem(2 + at.core * (n_z - 4), n_z))
    sources = [at.z_at(n_z - step)[0] for step in steps]
    pending = []
    for m in range(2):
        for j, step in enumerate(steps):
            copy = remote(channel_refs[m].at[:, pl.ds(at.x * n_k, n_k)], shard(m, at.dp, at.x),
                          f_send.at[m, j], f_recv.at[m, j], at.z_at(step))
            copy.start()
            pending.append(copy)
    own_factors = []
    for m in range(2):
        copy = pltpu.make_async_copy(channel_refs[m], shard(m, at.dp), local_sem.at[m])
        copy.start()
        own_factors.append(copy)

    l_step = 8 if n_l % 8 == 0 else 2

    def lookup(i, carry):
        dest = at.ctx_at(n_c - 1 - i)
        ids = ids_ref[:, pl.ds(pl.multiple_of(dest * block, block), block)]
        low, high = lax.rem(ids, block), ids // block
        hot = jnp.where(iota((block, block), 0) == low, 1.0, 0.0).astype(BF16)
        found = jnp.zeros((feats, block), F32)
        for start in range(0, n_l, l_step):
            picked = dot(tall[start * feats:(start + l_step) * feats, :], hot)
            for l in range(l_step):
                found = jnp.where(high == start + l, picked[l * feats:(l + 1) * feats], found)
        xa_send[dest] = jnp.concatenate([found[:, :half], found[:, half:]], axis=0).astype(BF16)

        @pl.when(i < n_c - 1)
        def _():
            remote(xa_send.at[dest], xa_recv.at[at.ctx], xa_sem.at[0], xa_sem.at[1],
                   (at.dp, dest)).start()

        @pl.when(i == n_c - 1)
        def _():
            pltpu.make_async_copy(xa_send.at[dest], xa_recv.at[at.ctx], xa_sem.at[1]).start()

        return carry

    def unpack():
        pltpu.make_async_copy(xa_recv, xa_recv, xa_sem.at[1]).wait()

        def flip(i, carry):
            both = xa_recv[i].astype(F32)
            start = pl.multiple_of(i * feats, feats)
            flipped[0, pl.ds(start, feats), :] = both[:feats]
            flipped[1, pl.ds(start, feats), :] = both[feats:]
            return carry

        lax.fori_loop(0, n_c, flip, 0)
        for i in range(2):
            for k in range(4):
                x_all[k, i * half:(i + 1) * half, :] = flipped[i, k * width:(k + 1) * width, :].T

    def norm_scale():
        square = jnp.zeros((block, 1), F32)
        for k in range(4):
            square = square + jnp.sum(x_all[k] * x_all[k], axis=1, keepdims=True)
        return lax.rsqrt(square / (4 * width) + 1e-06)

    def normed(m, k, scale):
        gain = gain_refs[m][k * width:(k + 1) * width].astype(F32).reshape(1, width)
        return (x_all[k] * scale * gain).astype(BF16)

    def send_part(send, recv, sems, first, last):
        def one(i, carry):
            dest = at.ctx_at(n_c - 1 - i)
            remote(send.at[dest // 2, lax.rem(dest, 2)],
                   recv.at[at.ctx // 2, lax.rem(at.ctx, 2)],
                   sems.at[0], sems.at[1], (at.dp, dest)).start()
            return carry

        lax.fori_loop(first, last, one, 0)

    def keep_own(send, recv, sems):
        pltpu.make_async_copy(send.at[at.ctx // 2, lax.rem(at.ctx, 2)],
                              recv.at[at.ctx // 2, lax.rem(at.ctx, 2)], sems.at[1]).start()

    def send_chunks(parts, send, recv, sems):
        to_chunks(parts, send)
        send_part(send, recv, sems, 0, n_c - 1)
        keep_own(send, recv, sems)

    lax.fori_loop(0, n_c, lookup, 0)

    for m in range(2):
        for j, source in enumerate(sources):
            remote(shard(m, source, at.x), shard(m, source, at.x), f_send.at[m, j],
                   f_recv.at[m, j], at.z_at(steps[j])).wait_recv()
            for o in range(1, at.n_x):
                copy = remote(shard(m, source, at.x), shard(m, source, at.x),
                              e_send.at[m, j, o - 1], e_recv.at[m, j, o - 1], at.x_peer(o))
                copy.start()
                pending.append(copy)

    unpack()
    send_chunks([x_all[k] for k in range(4)], xb_send, xb_recv, xb_sem)
    scale = norm_scale()
    for m in range(2):
        send_chunks([dot(blocks_refs[m][0], normed(m, k, scale)) for k in range(4)],
                    r_send.at[m], r_recv.at[m], r_sem.at[m])

    other = at.dp + 1 - 2 * at.core
    sibling = (other, at.ctx)
    for m in range(2):
        own_factors[m].wait()
        for j, source in enumerate([at.dp] + sources):
            if j:
                for o in range(1, at.n_x):
                    part = shard(m, source, lax.rem(at.x + at.n_x - o, at.n_x))
                    remote(part, part, e_send.at[m, j - 1, o - 1], e_recv.at[m, j - 1, o - 1],
                           at.x_peer(o)).wait_recv()
            copy = remote(shard(m, source), shard(m, source), g_send.at[m, j], g_recv.at[m, j],
                          sibling)
            copy.start()
            pending.append(copy)

    tall_one = jnp.where(iota((block, n_c), 0) // group == iota((block, n_c), 1), 1.0, 0.0)
    wide_one = jnp.where(iota((n_c, block), 1) // group == iota((n_c, block), 0), 1.0, 0.0)
    row_b, col_b = lax.rem(iota((block, block), 0), group), lax.rem(iota((block, block), 1), group)
    for m in range(2):
        total = jnp.zeros((block, block), F32)
        for b in range(group):
            piece = dot(dot(tall_one.astype(BF16), across_refs[m][b]).astype(BF16),
                        wide_one.astype(BF16))
            total = jnp.where((row_b == b) & (col_b == b), piece, total)
        mix[m] = total.astype(BF16)
    place, lane = iota((width, 4 * wide), 0), iota((width, 4 * wide), 1)
    inner = lax.rem(lane, wide)
    spread[...] = jnp.where(
        (place == (lane // wide) * quarter + inner) & (inner < quarter), 1.0, 0.0).astype(BF16)
    place, lane = iota((4 * wide, width), 0), iota((4 * wide, width), 1)
    inner = lax.rem(place, wide)
    gather[...] = jnp.where(
        (lane == inner * 4 + place // wide) & (inner < quarter), 1.0, 0.0).astype(BF16)

    pltpu.make_async_copy(xb_recv, xb_recv, xb_sem.at[1]).wait()
    parts = from_chunks(xb_recv)
    for k in range(4):
        x_all[k] = parts[k]
    scale = norm_scale()
    for m in range(2):
        for j in range(4):
            source = (at.dp if j == 0 else sources[j - 1]) + 1 - 2 * at.core
            remote(shard(m, source), shard(m, source), g_send.at[m, j], g_recv.at[m, j],
                   sibling).wait_recv()
        for k in range(4):
            first = dot(normed(m, k, scale), factors[m, 0, k]).astype(BF16)
            first = dot(first, spread[...]).astype(BF16)
            for q in range(4):
                padded[q, :, k * wide:(k + 1) * wide] = first[:, q * wide:(q + 1) * wide]
        for q in range(4):
            second = dot(gather[...], factors[m, 1, q]).astype(BF16)
            z = dot(padded[q], second)
            gates[m, q] = 1.0 / (1.0 + jnp.exp(-z))

    for m in range(2):
        pltpu.make_async_copy(r_recv.at[m], r_recv.at[m], r_sem.at[m, 1]).wait()
        parts = from_chunks(r_recv.at[m])
        outputs = []
        for k in range(4):
            mixed = dot(mix[m], parts[k].astype(BF16)).astype(BF16).astype(F32)
            y = (x_all[k] + mixed * gates[m, k]).astype(BF16).astype(F32)
            sums[m * 4 + k:m * 4 + k + 1, :] = jnp.sum(y, axis=0, keepdims=True)
            outputs.append(y)
        if m == 0:
            to_chunks(outputs, y_send)
            keep_own(y_send, y_recv, y_sem)
            send_part(y_send, y_recv, y_sem, 0, n_c // 8)

    stage = (sums, buf_y, send_y, recv_y, at.y_peer, at.y, at.n_y)
    pending += spread_out(*stage)
    send_part(y_send, y_recv, y_sem, n_c // 8, n_c // 8 * 3)
    gathered(*stage)
    own_y[...] = total_of(buf_y, at.n_y)
    stage = (own_y, buf_w, send_w, recv_w, at.w_peer, at.w, at.n_w)
    pending += spread_out(*stage)
    send_part(y_send, y_recv, y_sem, n_c // 8 * 3, n_c // 8 * 5)
    gathered(*stage)
    own_w[...] = total_of(buf_w, at.n_w) / seq_len
    stage = (own_w, buf_d, send_d, recv_d, at.d_peer, at.dp, n_d)
    pending += spread_out(*stage)
    send_part(y_send, y_recv, y_sem, n_c // 8 * 5, n_c // 8 * 7)
    gathered(*stage)
    local = []
    reps = n_d // 4
    for m in range(2):
        mine = (iota((8, 1), 0) == m * 4 + at.dp // reps).astype(F32)
        model = (iota((8, 1), 0) // 4 == m).astype(F32)
        rows, norms = [], []
        for n in range(n_d):
            pooled = buf_d[n]
            rows.append(jnp.sum(pooled * mine, axis=0, keepdims=True))
            square = jnp.sum(pooled * pooled * model, axis=0, keepdims=True)
            norms.append(jnp.sum(square, axis=1, keepdims=True))
        norm = lax.rsqrt(jnp.concatenate(norms, axis=0) / (4 * width) + 1e-06)
        head = head_refs[m][...].astype(F32)
        slot = iota((width, 1), 0) // (width // reps)
        head = jnp.where(slot == lax.rem(at.dp, reps), jnp.concatenate([head] * reps, axis=0), 0.0)
        local.append(jnp.dot(jnp.concatenate(rows, axis=0) * norm, head,
                             precision=lax.Precision.HIGHEST, preferred_element_type=F32))
    own_l[...] = jnp.concatenate(local, axis=1)
    stage = (own_l, buf_l, send_l, recv_l, at.d_peer, at.dp, n_d)
    pending += spread_out(*stage)
    send_part(y_send, y_recv, y_sem, n_c // 8 * 7, n_c - 1)
    gathered(*stage)
    logits = total_of(buf_l, n_d)
    classes = logits.shape[1] // 2
    row = iota((n_d, 1), 0)
    target = jnp.zeros((n_d, 1), jnp.int32)
    for n in range(n_d):
        target = jnp.where(row == n, target_ref[n], target)
    chosen = iota((n_d, classes), 1) == target
    losses = []
    for part in (logits[:, :classes], logits[:, classes:]):
        top = jnp.max(part, axis=1, keepdims=True)
        summed = jnp.log(jnp.sum(jnp.exp(part - top), axis=1, keepdims=True)) + top
        losses.append(summed - jnp.sum(jnp.where(chosen, part, 0.0), axis=1, keepdims=True))
    scores = losses[0] - losses[1]
    for n in range(n_d):
        score_ref[n] = jnp.sum(jnp.where(row == n, scores, 0.0))
    for k in range(candidate_ref.shape[0]):
        picked_ref[k] = jnp.sum(jnp.where(row == candidate_ref[k], scores, 0.0))

    pltpu.make_async_copy(y_recv, y_recv, y_sem.at[1]).wait()
    parts = from_chunks(y_recv)
    for k in range(4):
        out_ref[:, k * width:(k + 1) * width] = parts[k].astype(BF16)

    def sent(view, sem):
        pltpu.make_async_copy(view, view, sem).wait()

    sent(xa_send.at[pl.ds(0, n_c - 1)], xa_sem.at[0])
    for buf, sem in ((xb_send, xb_sem.at[0]), (r_send.at[0], r_sem.at[0, 0]),
                     (r_send.at[1], r_sem.at[1, 0]), (y_send, y_sem.at[0])):
        sent(buf.at[pl.ds(0, n_c // 2 - 1)], sem)
        sent(buf.at[0, 0], sem)
    for copy in pending:
        copy.wait_send()


def layer_call(ids, target, candidates, table, online, frozen, seq_len):
    n_d, n_c = lax.axis_size("dp"), lax.axis_size("ctx")
    n_x = 4 if n_c == 64 else n_c // 2
    n_w = 2 * n_x
    n_y = n_c // n_w
    feats, vocab = table.shape
    block = online[0].shape[1]
    depth, width = online[2].shape[2:]
    wide = -(-(width // 4) // 128) * 128
    n_l = -(-vocab // (2 * block)) * 2
    classes = online[4].shape[1]
    dma = pltpu.SemaphoreType.DMA
    found = (n_c, 2 * feats, block // 2)
    chunks = (n_c // 2, 2, 16, width)
    vmem, smem = pl.BlockSpec(memory_space=pltpu.VMEM), pl.BlockSpec(memory_space=pltpu.SMEM)
    return pl.pallas_call(
        functools.partial(layer_kernel, (n_d, n_c, seq_len)),
        out_shape=(jax.ShapeDtypeStruct((block, 4 * width), BF16),
                   jax.ShapeDtypeStruct((n_d,), F32),
                   jax.ShapeDtypeStruct(candidates.shape, F32)),
        in_specs=[vmem, smem, smem] + [vmem] * 11,
        out_specs=(vmem, smem, smem),
        scratch_shapes=[
            pltpu.VMEM((n_l * feats, block), BF16),
            pltpu.VMEM(found, BF16), pltpu.VMEM(found, BF16),
            pltpu.VMEM(chunks, BF16), pltpu.VMEM(chunks, BF16),
            pltpu.VMEM((2, n_c * feats, block // 2), F32),
            pltpu.VMEM((4, block, width), F32),
            pltpu.VMEM((2,) + chunks, BF16), pltpu.VMEM((2,) + chunks, BF16),
            pltpu.VMEM(chunks, BF16), pltpu.VMEM(chunks, BF16),
            pltpu.VMEM((2, 2, 4, depth * n_d, width), BF16),
            pltpu.VMEM((2, 4, block, width), F32),
            pltpu.VMEM((2, block, block), BF16),
            pltpu.VMEM((width, 4 * wide), BF16), pltpu.VMEM((4 * wide, width), BF16),
            pltpu.VMEM((4, block, 4 * wide), BF16),
            pltpu.VMEM((8, width), F32),
            pltpu.VMEM((n_y, 8, width), F32), pltpu.VMEM((n_w, 8, width), F32),
            pltpu.VMEM((n_d, 8, width), F32), pltpu.VMEM((n_d, n_d, 2 * classes), F32),
            pltpu.VMEM((8, width), F32), pltpu.VMEM((8, width), F32),
            pltpu.VMEM((n_d, 2 * classes), F32),
            dma((2,)), dma((2,)), dma((2, 2)), dma((2,)),
            dma((2, 3)), dma((2, 3)), dma((2, 3, max(n_x - 1, 1))), dma((2, 3, max(n_x - 1, 1))),
            dma((2, 4)), dma((2, 4)), dma((2,)),
            dma((n_y,)), dma((n_y,)), dma((n_w,)), dma((n_w,)),
            dma((n_d,)), dma((n_d,)), dma((n_d,)), dma((n_d,)),
        ],
        compiler_params=pltpu.CompilerParams(
            collective_id=1, has_side_effects=True, vmem_limit_bytes=56 * 1024 * 1024),
        name="layer",
    )(ids, target, candidates, table, *online, *frozen)


def body(
    token_ids,
    target_ids,
    candidates,
    embed_table,
    online_blocks,
    online_across,
    online_channel,
    online_gain,
    online_head,
    ref_blocks,
    ref_across,
    ref_channel,
    ref_gain,
    ref_head,
):
    return layer_call(
        token_ids,
        target_ids,
        candidates,
        embed_table,
        (online_blocks, online_across, online_channel, online_gain, online_head),
        (ref_blocks, ref_across, ref_channel, ref_gain, ref_head),
        token_ids.shape[1],
    )


def solution(mesh):
    in_specs = (
        P("dp", None),
        P(),
        P(),
        P("ctx", None),
        P("ctx", None, None),
        P("ctx", None, None),
        P(None, None, "dp", None),
        P(),
        P("dp", None),
        P("ctx", None, None),
        P("ctx", None, None),
        P(None, None, "dp", None),
        P(),
        P("dp", None),
    )
    out_specs = (P(("dp", "ctx"), None), P(), P())
    return jax.shard_map(body, mesh=mesh, in_specs=in_specs, out_specs=out_specs, check_vma=False)
```

```python
import functools
import jax
import jax.numpy as jnp
from jax import lax
from jax.experimental import pallas as pl
from jax.experimental.pallas import tpu as pltpu
from jax.sharding import PartitionSpec as P

MESH = pl.DeviceIdType.MESH
F32 = jnp.float32
BF16 = jnp.bfloat16
HALF_TILE = 4


def dot(a, b):
    return jnp.dot(a, b, preferred_element_type=F32)


def iota(shape, axis):
    return lax.broadcasted_iota(jnp.int32, shape, axis)


class Place:
    def __init__(self, n_d, n_c):
        self.n_d, self.n_c = n_d, n_c
        self.n_x = 4 if n_c == 64 else n_c // 2
        self.n_y = n_c // (2 * self.n_x)
        self.n_w = 2 * self.n_x
        self.z_lo_size = n_d // 2
        self.z_size = 2 * self.z_lo_size
        self.dp, self.ctx = lax.axis_index("dp"), lax.axis_index("ctx")
        self.y, self.w = self.ctx // self.n_w, lax.rem(self.ctx, self.n_w)
        self.z_hi, self.x = self.w // self.n_x, lax.rem(self.w, self.n_x)
        self.z_lo, self.core = self.dp // 2, lax.rem(self.dp, 2)
        self.z = self.z_hi * self.z_lo_size + self.z_lo

    def ctx_at(self, o):
        step_y = lax.rem(lax.rem(o, self.n_y) * 3, self.n_y)
        rest = o // self.n_y
        step_z, step_x = lax.rem(rest, 2), rest // 2
        y = lax.rem(self.y + step_y, self.n_y)
        z_hi = lax.rem(self.z_hi + step_z, 2)
        x = lax.rem(self.x + step_x, self.n_x)
        return y * self.n_w + z_hi * self.n_x + x

    def z_at(self, step):
        z = lax.rem(self.z + step, self.z_size)
        dp = lax.rem(z, self.z_lo_size) * 2 + self.core
        ctx = self.y * self.n_w + (z // self.z_lo_size) * self.n_x + self.x
        return dp, ctx

    def x_peer(self, o):
        x = lax.rem(self.x + o, self.n_x)
        return (self.dp, self.y * self.n_w + self.z_hi * self.n_x + x)

    def y_peer(self, o):
        return (self.dp, lax.rem(self.y + o, self.n_y) * self.n_w + self.w)

    def w_peer(self, o):
        return (self.dp, self.y * self.n_w + lax.rem(self.w + o, self.n_w))

    def d_peer(self, o):
        return (lax.rem(self.dp + o, self.n_d), self.ctx)


def remote(src, dst, send, recv, device):
    return pltpu.make_async_remote_copy(
        src_ref=src, dst_ref=dst, send_sem=send, recv_sem=recv,
        device_id=device, device_id_type=MESH)


def spread_out(own, buf, send, recv, peer, me, count):
    copies = []
    for o in range(1, count):
        copy = remote(own, buf.at[me], send.at[o], recv.at[me], peer(o))
        copy.start()
        copies.append(copy)
    buf[me] = own[...]
    return copies


def gathered(own, buf, send, recv, peer, me, count):
    for o in range(1, count):
        slot = lax.rem(me + o, count)
        remote(own, buf.at[slot], send.at[o], recv.at[slot], peer(o)).wait_recv()


def total_of(buf, count):
    total = buf[0]
    for j in range(1, count):
        total = total + buf[j]
    return total


def to_chunks(parts, ref):
    rows, width = parts[0].shape
    tiles = [p.reshape(rows // 8, 8, width) for p in parts]
    rolled = [pltpu.roll(t, HALF_TILE, 1) for t in tiles]
    upper = iota((1, 8, 1), 1) < HALF_TILE
    even = [jnp.where(upper, tiles[i], rolled[i + 1]) for i in (0, 2)]
    odd = [jnp.where(upper, rolled[i], tiles[i + 1]) for i in (0, 2)]
    ref[:, 0] = jnp.concatenate(even, axis=1).astype(BF16)
    ref[:, 1] = jnp.concatenate(odd, axis=1).astype(BF16)


def from_chunks(ref):
    even, odd = ref[:, 0].astype(F32), ref[:, 1].astype(F32)
    rows, width = even.shape[0] * 8, even.shape[2]
    upper = iota((1, 8, 1), 1) < HALF_TILE
    parts = []
    for i in (0, 1):
        e, o = even[:, 8 * i:8 * i + 8], odd[:, 8 * i:8 * i + 8]
        parts.append(jnp.where(upper, e, pltpu.roll(o, HALF_TILE, 1)).reshape(rows, width))
        parts.append(jnp.where(upper, pltpu.roll(e, HALF_TILE, 1), o).reshape(rows, width))
    return parts


def layer_kernel(
    dims, ids_ref, target_ref, candidate_ref, table_ref,
    online_blocks, online_across, online_channel, online_gain, online_head,
    frozen_blocks, frozen_across, frozen_channel, frozen_gain, frozen_head,
    out_ref, score_ref, picked_ref,
    tall, xa_send, xa_recv, xb_send, xb_recv, flipped, x_all, r_send, r_recv, y_send, y_recv,
    factors, gates, mix, spread, gather, padded, sums,
    buf_y, buf_w, buf_d, buf_l, own_y, own_w, own_l,
    xa_sem, xb_sem, r_sem, y_sem, f_send, f_recv, e_send, e_recv, g_send, g_recv, local_sem,
    send_y, recv_y, send_w, recv_w, send_d, recv_d, send_l, recv_l,
):
    n_d, n_c, seq_len = dims
    at = Place(n_d, n_c)
    blocks_refs = (online_blocks, frozen_blocks)
    across_refs = (online_across, frozen_across)
    channel_refs = (online_channel, frozen_channel)
    gain_refs = (online_gain, frozen_gain)
    head_refs = (online_head, frozen_head)
    feats, vocab = table_ref.shape
    block = online_blocks.shape[1]
    half = block // 2
    depth, width = online_channel.shape[2:]
    quarter = width // 4
    wide = gather.shape[0] // 4
    n_l = tall.shape[0] // feats
    n_z = at.z_size
    group = online_across.shape[0]

    barrier = pltpu.get_barrier_semaphore()

    def greet(o, carry):
        pl.semaphore_signal(barrier, inc=1, device_id=(at.dp, at.ctx_at(o)), device_id_type=MESH)
        return carry

    lax.fori_loop(1, n_c, greet, 0)
    for o in range(1, n_d):
        pl.semaphore_signal(barrier, inc=1, device_id=at.d_peer(o), device_id_type=MESH)
    for step in (1, 2, n_z - 2, n_z - 1):
        pl.semaphore_signal(barrier, inc=1, device_id=at.z_at(step), device_id_type=MESH)

    def tall_pair(i, carry):
        start = pl.multiple_of(i * 2 * block, 2 * block)
        pair = table_ref[:, pl.ds(start, 2 * block)].astype(F32)
        tall[pl.ds(pl.multiple_of(i * 2 * feats, 2 * feats), 2 * feats), :] = jnp.concatenate(
            [pair[:, :block], pair[:, block:]], axis=0).astype(BF16)
        return carry

    full = vocab // (2 * block)
    lax.fori_loop(0, full, tall_pair, 0)
    if full * 2 < n_l:
        left = table_ref[:, full * 2 * block:].astype(F32)
        left = jnp.concatenate(
            [left, jnp.zeros((feats, 2 * block - left.shape[1]), F32)], axis=1)
        tall[full * 2 * feats:, :] = jnp.concatenate(
            [left[:, :block], left[:, block:]], axis=0).astype(BF16)

    pl.semaphore_wait(barrier, n_c - 1 + n_d - 1 + 4)

    n_k = 4 // at.n_x

    def shard(m, dp, x=None):
        rows = pl.ds(pl.multiple_of(dp * depth, depth), depth)
        if x is None:
            return factors.at[m, :, :, rows, :]
        return factors.at[m, :, pl.ds(x * n_k, n_k), rows, :]

    steps = (1, n_z - 1, lax.rem(2 + at.core * (n_z - 4), n_z))
    sources = [at.z_at(n_z - step)[0] for step in steps]
    pending = []
    for m in range(2):
        for j, step in enumerate(steps):
            copy = remote(channel_refs[m].at[:, pl.ds(at.x * n_k, n_k)], shard(m, at.dp, at.x),
                          f_send.at[m, j], f_recv.at[m, j], at.z_at(step))
            copy.start()
            pending.append(copy)
    own_factors = []
    for m in range(2):
        copy = pltpu.make_async_copy(channel_refs[m], shard(m, at.dp), local_sem.at[m])
        copy.start()
        own_factors.append(copy)

    l_step = 8 if n_l % 8 == 0 else 2
    per_step = 2

    def lookup(i, carry):
        dests = [at.ctx_at(n_c - 1 - (i * per_step + j)) for j in range(per_step)]
        ids = jnp.concatenate(
            [ids_ref[:, pl.ds(pl.multiple_of(d * block, block), block)] for d in dests], axis=1)
        low, high = lax.rem(ids, block), ids // block
        hot = jnp.where(iota((block, per_step * block), 0) == low, 1.0, 0.0).astype(BF16)
        found = jnp.zeros((feats, per_step * block), F32)
        for start in range(0, n_l, l_step):
            picked = dot(tall[start * feats:(start + l_step) * feats, :], hot)
            for l in range(l_step):
                found = jnp.where(high == start + l, picked[l * feats:(l + 1) * feats], found)
        for j, dest in enumerate(dests):
            mine = found[:, j * block:(j + 1) * block]
            xa_send[dest] = jnp.concatenate([mine[:, :half], mine[:, half:]], axis=0).astype(BF16)

            def send(dest=dest):
                remote(xa_send.at[dest], xa_recv.at[at.ctx], xa_sem.at[0], xa_sem.at[1],
                       (at.dp, dest)).start()

            if j < per_step - 1:
                send()
            else:
                pl.when(i < n_c // per_step - 1)(send)

                @pl.when(i == n_c // per_step - 1)
                def _():
                    pltpu.make_async_copy(
                        xa_send.at[dest], xa_recv.at[at.ctx], xa_sem.at[1]).start()

        return carry

    def unpack():
        pltpu.make_async_copy(xa_recv, xa_recv, xa_sem.at[1]).wait()

        def flip(i, carry):
            both = xa_recv[i].astype(F32)
            start = pl.multiple_of(i * feats, feats)
            flipped[0, pl.ds(start, feats), :] = both[:feats]
            flipped[1, pl.ds(start, feats), :] = both[feats:]
            return carry

        lax.fori_loop(0, n_c, flip, 0)
        for i in range(2):
            for k in range(4):
                x_all[k, i * half:(i + 1) * half, :] = flipped[i, k * width:(k + 1) * width, :].T

    def norm_scale():
        square = jnp.zeros((block, 1), F32)
        for k in range(4):
            square = square + jnp.sum(x_all[k] * x_all[k], axis=1, keepdims=True)
        return lax.rsqrt(square / (4 * width) + 1e-06)

    def normed(m, k, scale):
        gain = gain_refs[m][k * width:(k + 1) * width].astype(F32).reshape(1, width)
        return (x_all[k] * scale * gain).astype(BF16)

    def send_part(send, recv, sems, first, last):
        def one(i, carry):
            dest = at.ctx_at(n_c - 1 - i)
            remote(send.at[dest // 2, lax.rem(dest, 2)],
                   recv.at[at.ctx // 2, lax.rem(at.ctx, 2)],
                   sems.at[0], sems.at[1], (at.dp, dest)).start()
            return carry

        lax.fori_loop(first, last, one, 0)

    def keep_own(send, recv, sems):
        pltpu.make_async_copy(send.at[at.ctx // 2, lax.rem(at.ctx, 2)],
                              recv.at[at.ctx // 2, lax.rem(at.ctx, 2)], sems.at[1]).start()

    def send_chunks(parts, send, recv, sems):
        to_chunks(parts, send)
        send_part(send, recv, sems, 0, n_c - 1)
        keep_own(send, recv, sems)

    n_steps = n_c // per_step
    first_stop, second_stop = n_steps // 4, n_steps * 7 // 8
    lax.fori_loop(0, first_stop, lookup, 0)

    for m in range(2):
        for j, source in enumerate(sources):
            remote(shard(m, source, at.x), shard(m, source, at.x), f_send.at[m, j],
                   f_recv.at[m, j], at.z_at(steps[j])).wait_recv()
            for o in range(1, at.n_x):
                copy = remote(shard(m, source, at.x), shard(m, source, at.x),
                              e_send.at[m, j, o - 1], e_recv.at[m, j, o - 1], at.x_peer(o))
                copy.start()
                pending.append(copy)

    lax.fori_loop(first_stop, second_stop, lookup, 0)

    other = at.dp + 1 - 2 * at.core
    sibling = (other, at.ctx)
    for m in range(2):
        own_factors[m].wait()
        for j, source in enumerate([at.dp] + sources):
            if j:
                for o in range(1, at.n_x):
                    part = shard(m, source, lax.rem(at.x + at.n_x - o, at.n_x))
                    remote(part, part, e_send.at[m, j - 1, o - 1], e_recv.at[m, j - 1, o - 1],
                           at.x_peer(o)).wait_recv()
            copy = remote(shard(m, source), shard(m, source), g_send.at[m, j], g_recv.at[m, j],
                          sibling)
            copy.start()
            pending.append(copy)

    lax.fori_loop(second_stop, n_steps, lookup, 0)

    unpack()
    send_chunks([x_all[k] for k in range(4)], xb_send, xb_recv, xb_sem)
    scale = norm_scale()
    for m in range(2):
        send_chunks([dot(blocks_refs[m][0], normed(m, k, scale)) for k in range(4)],
                    r_send.at[m], r_recv.at[m], r_sem.at[m])

    tall_one = jnp.where(iota((block, n_c), 0) // group == iota((block, n_c), 1), 1.0, 0.0)
    wide_one = jnp.where(iota((n_c, block), 1) // group == iota((n_c, block), 0), 1.0, 0.0)
    row_b, col_b = lax.rem(iota((block, block), 0), group), lax.rem(iota((block, block), 1), group)
    for m in range(2):
        total = jnp.zeros((block, block), F32)
        for b in range(group):
            piece = dot(dot(tall_one.astype(BF16), across_refs[m][b]).astype(BF16),
                        wide_one.astype(BF16))
            total = jnp.where((row_b == b) & (col_b == b), piece, total)
        mix[m] = total.astype(BF16)
    place, lane = iota((width, 4 * wide), 0), iota((width, 4 * wide), 1)
    inner = lax.rem(lane, wide)
    spread[...] = jnp.where(
        (place == (lane // wide) * quarter + inner) & (inner < quarter), 1.0, 0.0).astype(BF16)
    place, lane = iota((4 * wide, width), 0), iota((4 * wide, width), 1)
    inner = lax.rem(place, wide)
    gather[...] = jnp.where(
        (lane == inner * 4 + place // wide) & (inner < quarter), 1.0, 0.0).astype(BF16)

    pltpu.make_async_copy(xb_recv, xb_recv, xb_sem.at[1]).wait()
    parts = from_chunks(xb_recv)
    for k in range(4):
        x_all[k] = parts[k]
    scale = norm_scale()
    for m in range(2):
        for j in range(4):
            source = (at.dp if j == 0 else sources[j - 1]) + 1 - 2 * at.core
            remote(shard(m, source), shard(m, source), g_send.at[m, j], g_recv.at[m, j],
                   sibling).wait_recv()
        for k in range(4):
            first = dot(normed(m, k, scale), factors[m, 0, k]).astype(BF16)
            first = dot(first, spread[...]).astype(BF16)
            for q in range(4):
                padded[q, :, k * wide:(k + 1) * wide] = first[:, q * wide:(q + 1) * wide]
        for q in range(4):
            second = dot(gather[...], factors[m, 1, q]).astype(BF16)
            z = dot(padded[q], second)
            gates[m, q] = 1.0 / (1.0 + jnp.exp(-z))

    for m in range(2):
        pltpu.make_async_copy(r_recv.at[m], r_recv.at[m], r_sem.at[m, 1]).wait()
        parts = from_chunks(r_recv.at[m])
        outputs = []
        for k in range(4):
            mixed = dot(mix[m], parts[k].astype(BF16)).astype(BF16).astype(F32)
            y = (x_all[k] + mixed * gates[m, k]).astype(BF16).astype(F32)
            sums[m * 4 + k:m * 4 + k + 1, :] = jnp.sum(y, axis=0, keepdims=True)
            outputs.append(y)
        if m == 0:
            to_chunks(outputs, y_send)
            keep_own(y_send, y_recv, y_sem)
            send_part(y_send, y_recv, y_sem, 0, n_c // 8 * 3)

    stage = (sums, buf_y, send_y, recv_y, at.y_peer, at.y, at.n_y)
    pending += spread_out(*stage)
    send_part(y_send, y_recv, y_sem, n_c // 8 * 3, n_c // 8 * 5)
    gathered(*stage)
    own_y[...] = total_of(buf_y, at.n_y)
    stage = (own_y, buf_w, send_w, recv_w, at.w_peer, at.w, at.n_w)
    pending += spread_out(*stage)
    send_part(y_send, y_recv, y_sem, n_c // 8 * 5, n_c // 8 * 6)
    gathered(*stage)
    own_w[...] = total_of(buf_w, at.n_w) / seq_len
    stage = (own_w, buf_d, send_d, recv_d, at.d_peer, at.dp, n_d)
    pending += spread_out(*stage)
    send_part(y_send, y_recv, y_sem, n_c // 8 * 6, n_c // 8 * 7)
    gathered(*stage)
    local = []
    reps = n_d // 4
    for m in range(2):
        mine = (iota((8, 1), 0) == m * 4 + at.dp // reps).astype(F32)
        model = (iota((8, 1), 0) // 4 == m).astype(F32)
        rows, norms = [], []
        for n in range(n_d):
            pooled = buf_d[n]
            rows.append(jnp.sum(pooled * mine, axis=0, keepdims=True))
            square = jnp.sum(pooled * pooled * model, axis=0, keepdims=True)
            norms.append(jnp.sum(square, axis=1, keepdims=True))
        norm = lax.rsqrt(jnp.concatenate(norms, axis=0) / (4 * width) + 1e-06)
        head = head_refs[m][...].astype(F32)
        slot = iota((width, 1), 0) // (width // reps)
        head = jnp.where(slot == lax.rem(at.dp, reps), jnp.concatenate([head] * reps, axis=0), 0.0)
        local.append(jnp.dot(jnp.concatenate(rows, axis=0) * norm, head,
                             precision=lax.Precision.HIGHEST, preferred_element_type=F32))
    own_l[...] = jnp.concatenate(local, axis=1)
    stage = (own_l, buf_l, send_l, recv_l, at.d_peer, at.dp, n_d)
    pending += spread_out(*stage)
    send_part(y_send, y_recv, y_sem, n_c // 8 * 7, n_c - 1)
    gathered(*stage)
    logits = total_of(buf_l, n_d)
    classes = logits.shape[1] // 2
    row = iota((n_d, 1), 0)
    target = jnp.zeros((n_d, 1), jnp.int32)
    for n in range(n_d):
        target = jnp.where(row == n, target_ref[n], target)
    chosen = iota((n_d, classes), 1) == target
    losses = []
    for part in (logits[:, :classes], logits[:, classes:]):
        top = jnp.max(part, axis=1, keepdims=True)
        summed = jnp.log(jnp.sum(jnp.exp(part - top), axis=1, keepdims=True)) + top
        losses.append(summed - jnp.sum(jnp.where(chosen, part, 0.0), axis=1, keepdims=True))
    scores = losses[0] - losses[1]
    for n in range(n_d):
        score_ref[n] = jnp.sum(jnp.where(row == n, scores, 0.0))
    for k in range(candidate_ref.shape[0]):
        picked_ref[k] = jnp.sum(jnp.where(row == candidate_ref[k], scores, 0.0))

    pltpu.make_async_copy(y_recv, y_recv, y_sem.at[1]).wait()
    parts = from_chunks(y_recv)
    for k in range(4):
        out_ref[:, k * width:(k + 1) * width] = parts[k].astype(BF16)

    def sent(view, sem):
        pltpu.make_async_copy(view, view, sem).wait()

    sent(xa_send.at[pl.ds(0, n_c - 1)], xa_sem.at[0])
    for buf, sem in ((xb_send, xb_sem.at[0]), (r_send.at[0], r_sem.at[0, 0]),
                     (r_send.at[1], r_sem.at[1, 0]), (y_send, y_sem.at[0])):
        sent(buf.at[pl.ds(0, n_c // 2 - 1)], sem)
        sent(buf.at[0, 0], sem)
    for copy in pending:
        copy.wait_send()


def layer_call(ids, target, candidates, table, online, frozen, seq_len):
    n_d, n_c = lax.axis_size("dp"), lax.axis_size("ctx")
    n_x = 4 if n_c == 64 else n_c // 2
    n_w = 2 * n_x
    n_y = n_c // n_w
    feats, vocab = table.shape
    block = online[0].shape[1]
    depth, width = online[2].shape[2:]
    wide = -(-(width // 4) // 128) * 128
    n_l = -(-vocab // (2 * block)) * 2
    classes = online[4].shape[1]
    dma = pltpu.SemaphoreType.DMA
    found = (n_c, 2 * feats, block // 2)
    chunks = (n_c // 2, 2, 16, width)
    vmem, smem = pl.BlockSpec(memory_space=pltpu.VMEM), pl.BlockSpec(memory_space=pltpu.SMEM)
    return pl.pallas_call(
        functools.partial(layer_kernel, (n_d, n_c, seq_len)),
        out_shape=(jax.ShapeDtypeStruct((block, 4 * width), BF16),
                   jax.ShapeDtypeStruct((n_d,), F32),
                   jax.ShapeDtypeStruct(candidates.shape, F32)),
        in_specs=[vmem, smem, smem] + [vmem] * 11,
        out_specs=(vmem, smem, smem),
        scratch_shapes=[
            pltpu.VMEM((n_l * feats, block), BF16),
            pltpu.VMEM(found, BF16), pltpu.VMEM(found, BF16),
            pltpu.VMEM(chunks, BF16), pltpu.VMEM(chunks, BF16),
            pltpu.VMEM((2, n_c * feats, block // 2), F32),
            pltpu.VMEM((4, block, width), F32),
            pltpu.VMEM((2,) + chunks, BF16), pltpu.VMEM((2,) + chunks, BF16),
            pltpu.VMEM(chunks, BF16), pltpu.VMEM(chunks, BF16),
            pltpu.VMEM((2, 2, 4, depth * n_d, width), BF16),
            pltpu.VMEM((2, 4, block, width), F32),
            pltpu.VMEM((2, block, block), BF16),
            pltpu.VMEM((width, 4 * wide), BF16), pltpu.VMEM((4 * wide, width), BF16),
            pltpu.VMEM((4, block, 4 * wide), BF16),
            pltpu.VMEM((8, width), F32),
            pltpu.VMEM((n_y, 8, width), F32), pltpu.VMEM((n_w, 8, width), F32),
            pltpu.VMEM((n_d, 8, width), F32), pltpu.VMEM((n_d, n_d, 2 * classes), F32),
            pltpu.VMEM((8, width), F32), pltpu.VMEM((8, width), F32),
            pltpu.VMEM((n_d, 2 * classes), F32),
            dma((2,)), dma((2,)), dma((2, 2)), dma((2,)),
            dma((2, 3)), dma((2, 3)), dma((2, 3, max(n_x - 1, 1))), dma((2, 3, max(n_x - 1, 1))),
            dma((2, 4)), dma((2, 4)), dma((2,)),
            dma((n_y,)), dma((n_y,)), dma((n_w,)), dma((n_w,)),
            dma((n_d,)), dma((n_d,)), dma((n_d,)), dma((n_d,)),
        ],
        compiler_params=pltpu.CompilerParams(
            collective_id=1, has_side_effects=True, vmem_limit_bytes=56 * 1024 * 1024),
        name="layer",
    )(ids, target, candidates, table, *online, *frozen)


def body(
    token_ids,
    target_ids,
    candidates,
    embed_table,
    online_blocks,
    online_across,
    online_channel,
    online_gain,
    online_head,
    ref_blocks,
    ref_across,
    ref_channel,
    ref_gain,
    ref_head,
):
    return layer_call(
        token_ids,
        target_ids,
        candidates,
        embed_table,
        (online_blocks, online_across, online_channel, online_gain, online_head),
        (ref_blocks, ref_across, ref_channel, ref_gain, ref_head),
        token_ids.shape[1],
    )


def solution(mesh):
    in_specs = (
        P("dp", None),
        P(),
        P(),
        P("ctx", None),
        P("ctx", None, None),
        P("ctx", None, None),
        P(None, None, "dp", None),
        P(),
        P("dp", None),
        P("ctx", None, None),
        P("ctx", None, None),
        P(None, None, "dp", None),
        P(),
        P("dp", None),
    )
    out_specs = (P(("dp", "ctx"), None), P(), P())
    return jax.shard_map(body, mesh=mesh, in_specs=in_specs, out_specs=out_specs, check_vma=False)
```

```python
import functools
import jax
import jax.numpy as jnp
from jax import lax
from jax.experimental import pallas as pl
from jax.experimental.pallas import tpu as pltpu
from jax.sharding import PartitionSpec as P

MESH = pl.DeviceIdType.MESH
F32 = jnp.float32
BF16 = jnp.bfloat16
HALF_TILE = 4


def dot(a, b):
    return jnp.dot(a, b, preferred_element_type=F32)


def iota(shape, axis):
    return lax.broadcasted_iota(jnp.int32, shape, axis)


class Place:
    def __init__(self, n_d, n_c):
        self.n_d, self.n_c = n_d, n_c
        self.n_x = 4 if n_c == 64 else n_c // 2
        self.n_y = n_c // (2 * self.n_x)
        self.n_w = 2 * self.n_x
        self.z_lo_size = n_d // 2
        self.z_size = 2 * self.z_lo_size
        self.dp, self.ctx = lax.axis_index("dp"), lax.axis_index("ctx")
        self.y, self.w = self.ctx // self.n_w, lax.rem(self.ctx, self.n_w)
        self.z_hi, self.x = self.w // self.n_x, lax.rem(self.w, self.n_x)
        self.z_lo, self.core = self.dp // 2, lax.rem(self.dp, 2)
        self.z = self.z_hi * self.z_lo_size + self.z_lo

    def ctx_at(self, o):
        step_y = lax.rem(lax.rem(o, self.n_y) * 3, self.n_y)
        rest = o // self.n_y
        step_z, step_x = lax.rem(rest, 2), rest // 2
        y = lax.rem(self.y + step_y, self.n_y)
        z_hi = lax.rem(self.z_hi + step_z, 2)
        x = lax.rem(self.x + step_x, self.n_x)
        return y * self.n_w + z_hi * self.n_x + x

    def z_at(self, step):
        z = lax.rem(self.z + step, self.z_size)
        dp = lax.rem(z, self.z_lo_size) * 2 + self.core
        ctx = self.y * self.n_w + (z // self.z_lo_size) * self.n_x + self.x
        return dp, ctx

    def x_peer(self, o):
        x = lax.rem(self.x + o, self.n_x)
        return (self.dp, self.y * self.n_w + self.z_hi * self.n_x + x)

    def y_peer(self, o):
        return (self.dp, lax.rem(self.y + o, self.n_y) * self.n_w + self.w)

    def w_peer(self, o):
        return (self.dp, self.y * self.n_w + lax.rem(self.w + o, self.n_w))

    def d_peer(self, o):
        return (lax.rem(self.dp + o, self.n_d), self.ctx)


def remote(src, dst, send, recv, device):
    return pltpu.make_async_remote_copy(
        src_ref=src, dst_ref=dst, send_sem=send, recv_sem=recv,
        device_id=device, device_id_type=MESH)


def spread_out(own, buf, send, recv, peer, me, count):
    copies = []
    for o in range(1, count):
        copy = remote(own, buf.at[me], send.at[o], recv.at[me], peer(o))
        copy.start()
        copies.append(copy)
    buf[me] = own[...]
    return copies


def gathered(own, buf, send, recv, peer, me, count):
    for o in range(1, count):
        slot = lax.rem(me + o, count)
        remote(own, buf.at[slot], send.at[o], recv.at[slot], peer(o)).wait_recv()


def total_of(buf, count):
    total = buf[0]
    for j in range(1, count):
        total = total + buf[j]
    return total


def to_chunks(parts, ref):
    rows, width = parts[0].shape
    tiles = [p.reshape(rows // 8, 8, width) for p in parts]
    rolled = [pltpu.roll(t, HALF_TILE, 1) for t in tiles]
    upper = iota((1, 8, 1), 1) < HALF_TILE
    even = [jnp.where(upper, tiles[i], rolled[i + 1]) for i in (0, 2)]
    odd = [jnp.where(upper, rolled[i], tiles[i + 1]) for i in (0, 2)]
    ref[:, 0] = jnp.concatenate(even, axis=1).astype(BF16)
    ref[:, 1] = jnp.concatenate(odd, axis=1).astype(BF16)


def from_chunks(ref):
    even, odd = ref[:, 0].astype(F32), ref[:, 1].astype(F32)
    rows, width = even.shape[0] * 8, even.shape[2]
    upper = iota((1, 8, 1), 1) < HALF_TILE
    parts = []
    for i in (0, 1):
        e, o = even[:, 8 * i:8 * i + 8], odd[:, 8 * i:8 * i + 8]
        parts.append(jnp.where(upper, e, pltpu.roll(o, HALF_TILE, 1)).reshape(rows, width))
        parts.append(jnp.where(upper, pltpu.roll(e, HALF_TILE, 1), o).reshape(rows, width))
    return parts


def layer_kernel(
    dims, ids_ref, target_ref, candidate_ref, table_ref,
    online_blocks, online_across, online_channel, online_gain, online_head,
    frozen_blocks, frozen_across, frozen_channel, frozen_gain, frozen_head,
    out_ref, score_ref, picked_ref,
    tall, xa_send, xa_recv, xb_send, xb_recv, flipped, x_all, r_send, r_recv, y_send, y_recv,
    factors, gates, mix, spread, gather, padded, sums,
    buf_y, buf_w, buf_d, buf_l, own_y, own_w, own_l,
    xa_sem, xb_sem, r_sem, y_sem, f_send, f_recv, e_send, e_recv, g_send, g_recv, local_sem,
    send_y, recv_y, send_w, recv_w, send_d, recv_d, send_l, recv_l,
):
    n_d, n_c, seq_len = dims
    at = Place(n_d, n_c)
    blocks_refs = (online_blocks, frozen_blocks)
    across_refs = (online_across, frozen_across)
    channel_refs = (online_channel, frozen_channel)
    gain_refs = (online_gain, frozen_gain)
    head_refs = (online_head, frozen_head)
    feats, vocab = table_ref.shape
    block = online_blocks.shape[1]
    half = block // 2
    depth, width = online_channel.shape[2:]
    quarter = width // 4
    wide = gather.shape[0] // 4
    n_l = tall.shape[0] // feats
    n_z = at.z_size
    group = online_across.shape[0]

    barrier = pltpu.get_barrier_semaphore()

    def greet(o, carry):
        pl.semaphore_signal(barrier, inc=1, device_id=(at.dp, at.ctx_at(o)), device_id_type=MESH)
        return carry

    lax.fori_loop(1, n_c, greet, 0)
    for o in range(1, n_d):
        pl.semaphore_signal(barrier, inc=1, device_id=at.d_peer(o), device_id_type=MESH)
    for step in (1, 2, n_z - 2, n_z - 1):
        pl.semaphore_signal(barrier, inc=1, device_id=at.z_at(step), device_id_type=MESH)

    def tall_pair(i, carry):
        start = pl.multiple_of(i * 2 * block, 2 * block)
        pair = table_ref[:, pl.ds(start, 2 * block)].astype(F32)
        tall[pl.ds(pl.multiple_of(i * 2 * feats, 2 * feats), 2 * feats), :] = jnp.concatenate(
            [pair[:, :block], pair[:, block:]], axis=0).astype(BF16)
        return carry

    full = vocab // (2 * block)
    lax.fori_loop(0, full, tall_pair, 0)
    if full * 2 < n_l:
        left = table_ref[:, full * 2 * block:].astype(F32)
        left = jnp.concatenate(
            [left, jnp.zeros((feats, 2 * block - left.shape[1]), F32)], axis=1)
        tall[full * 2 * feats:, :] = jnp.concatenate(
            [left[:, :block], left[:, block:]], axis=0).astype(BF16)

    n_k = 4 // at.n_x

    def shard(m, dp, x=None):
        rows = pl.ds(pl.multiple_of(dp * depth, depth), depth)
        if x is None:
            return factors.at[m, :, :, rows, :]
        return factors.at[m, :, pl.ds(x * n_k, n_k), rows, :]

    steps = (1, n_z - 1, lax.rem(2 + at.core * (n_z - 4), n_z))
    sources = [at.z_at(n_z - step)[0] for step in steps]
    pending = []
    own_factors = []
    for m in range(2):
        copy = pltpu.make_async_copy(channel_refs[m], shard(m, at.dp), local_sem.at[m])
        copy.start()
        own_factors.append(copy)

    l_step = 8 if n_l % 8 == 0 else 2
    per_step = 2

    def send_found(i):
        dest = at.ctx_at(n_c - 1 - i)

        @pl.when(i < n_c - 1)
        def _():
            remote(xa_send.at[dest], xa_recv.at[at.ctx], xa_sem.at[0], xa_sem.at[1],
                   (at.dp, dest)).start()

        @pl.when(i == n_c - 1)
        def _():
            pltpu.make_async_copy(xa_send.at[dest], xa_recv.at[at.ctx], xa_sem.at[1]).start()

    def send_early(i, carry):
        send_found(i)
        return carry

    def lookup(i, carry, sending=True):
        dests = [at.ctx_at(n_c - 1 - (i * per_step + j)) for j in range(per_step)]
        ids = jnp.concatenate(
            [ids_ref[:, pl.ds(pl.multiple_of(d * block, block), block)] for d in dests], axis=1)
        low, high = lax.rem(ids, block), ids // block
        hot = jnp.where(iota((block, per_step * block), 0) == low, 1.0, 0.0).astype(BF16)
        found = jnp.zeros((feats, per_step * block), F32)
        for start in range(0, n_l, l_step):
            picked = dot(tall[start * feats:(start + l_step) * feats, :], hot)
            for l in range(l_step):
                found = jnp.where(high == start + l, picked[l * feats:(l + 1) * feats], found)
        for j, dest in enumerate(dests):
            mine = found[:, j * block:(j + 1) * block]
            xa_send[dest] = jnp.concatenate([mine[:, :half], mine[:, half:]], axis=0).astype(BF16)

            if sending:
                send_found(i * per_step + j)

        return carry

    def unpack():
        pltpu.make_async_copy(xa_recv, xa_recv, xa_sem.at[1]).wait()

        def flip(i, carry):
            both = xa_recv[i].astype(F32)
            start = pl.multiple_of(i * feats, feats)
            flipped[0, pl.ds(start, feats), :] = both[:feats]
            flipped[1, pl.ds(start, feats), :] = both[feats:]
            return carry

        lax.fori_loop(0, n_c, flip, 0)
        for i in range(2):
            for k in range(4):
                x_all[k, i * half:(i + 1) * half, :] = flipped[i, k * width:(k + 1) * width, :].T

    def norm_scale():
        square = jnp.zeros((block, 1), F32)
        for k in range(4):
            square = square + jnp.sum(x_all[k] * x_all[k], axis=1, keepdims=True)
        return lax.rsqrt(square / (4 * width) + 1e-06)

    def normed(m, k, scale):
        gain = gain_refs[m][k * width:(k + 1) * width].astype(F32).reshape(1, width)
        return (x_all[k] * scale * gain).astype(BF16)

    def send_part(send, recv, sems, first, last):
        def one(i, carry):
            dest = at.ctx_at(n_c - 1 - i)
            remote(send.at[dest // 2, lax.rem(dest, 2)],
                   recv.at[at.ctx // 2, lax.rem(at.ctx, 2)],
                   sems.at[0], sems.at[1], (at.dp, dest)).start()
            return carry

        lax.fori_loop(first, last, one, 0)

    def keep_own(send, recv, sems):
        pltpu.make_async_copy(send.at[at.ctx // 2, lax.rem(at.ctx, 2)],
                              recv.at[at.ctx // 2, lax.rem(at.ctx, 2)], sems.at[1]).start()

    def send_chunks(parts, send, recv, sems):
        to_chunks(parts, send)
        send_part(send, recv, sems, 0, n_c - 1)
        keep_own(send, recv, sems)

    n_steps = n_c // per_step
    early = n_steps // 2

    lax.fori_loop(0, early, functools.partial(lookup, sending=False), 0)
    pl.semaphore_wait(barrier, n_c - 1 + n_d - 1 + 4)
    lax.fori_loop(0, early * per_step, send_early, 0)
    lax.fori_loop(early, n_steps, lookup, 0)

    for m in range(2):
        for j, step in enumerate(steps):
            copy = remote(channel_refs[m].at[:, pl.ds(at.x * n_k, n_k)], shard(m, at.dp, at.x),
                          f_send.at[m, j], f_recv.at[m, j], at.z_at(step))
            copy.start()
            pending.append(copy)

    unpack()
    send_chunks([x_all[k] for k in range(4)], xb_send, xb_recv, xb_sem)
    for m in range(2):
        for j, source in enumerate(sources):
            remote(shard(m, source, at.x), shard(m, source, at.x), f_send.at[m, j],
                   f_recv.at[m, j], at.z_at(steps[j])).wait_recv()
            for o in range(1, at.n_x):
                copy = remote(shard(m, source, at.x), shard(m, source, at.x),
                              e_send.at[m, j, o - 1], e_recv.at[m, j, o - 1], at.x_peer(o))
                copy.start()
                pending.append(copy)

    scale = norm_scale()
    def within(m):
        send_chunks([dot(blocks_refs[m][0], normed(m, k, scale)) for k in range(4)],
                    r_send.at[m], r_recv.at[m], r_sem.at[m])

    within(0)

    other = at.dp + 1 - 2 * at.core
    sibling = (other, at.ctx)
    for m in range(2):
        own_factors[m].wait()
        for j, source in enumerate([at.dp] + sources):
            if j:
                for o in range(1, at.n_x):
                    part = shard(m, source, lax.rem(at.x + at.n_x - o, at.n_x))
                    remote(part, part, e_send.at[m, j - 1, o - 1], e_recv.at[m, j - 1, o - 1],
                           at.x_peer(o)).wait_recv()
            copy = remote(shard(m, source), shard(m, source), g_send.at[m, j], g_recv.at[m, j],
                          sibling)
            copy.start()
            pending.append(copy)

    within(1)


    tall_one = jnp.where(iota((block, n_c), 0) // group == iota((block, n_c), 1), 1.0, 0.0)
    wide_one = jnp.where(iota((n_c, block), 1) // group == iota((n_c, block), 0), 1.0, 0.0)
    row_b, col_b = lax.rem(iota((block, block), 0), group), lax.rem(iota((block, block), 1), group)
    for m in range(2):
        total = jnp.zeros((block, block), F32)
        for b in range(group):
            piece = dot(dot(tall_one.astype(BF16), across_refs[m][b]).astype(BF16),
                        wide_one.astype(BF16))
            total = jnp.where((row_b == b) & (col_b == b), piece, total)
        mix[m] = total.astype(BF16)
    place, lane = iota((width, 4 * wide), 0), iota((width, 4 * wide), 1)
    inner = lax.rem(lane, wide)
    spread[...] = jnp.where(
        (place == (lane // wide) * quarter + inner) & (inner < quarter), 1.0, 0.0).astype(BF16)
    place, lane = iota((4 * wide, width), 0), iota((4 * wide, width), 1)
    inner = lax.rem(place, wide)
    gather[...] = jnp.where(
        (lane == inner * 4 + place // wide) & (inner < quarter), 1.0, 0.0).astype(BF16)

    pltpu.make_async_copy(xb_recv, xb_recv, xb_sem.at[1]).wait()
    parts = from_chunks(xb_recv)
    for k in range(4):
        x_all[k] = parts[k]
    scale = norm_scale()
    for m in range(2):
        for j in range(4):
            source = (at.dp if j == 0 else sources[j - 1]) + 1 - 2 * at.core
            remote(shard(m, source), shard(m, source), g_send.at[m, j], g_recv.at[m, j],
                   sibling).wait_recv()
        for k in range(4):
            first = dot(normed(m, k, scale), factors[m, 0, k]).astype(BF16)
            first = dot(first, spread[...]).astype(BF16)
            for q in range(4):
                padded[q, :, k * wide:(k + 1) * wide] = first[:, q * wide:(q + 1) * wide]
        for q in range(4):
            second = dot(gather[...], factors[m, 1, q]).astype(BF16)
            z = dot(padded[q], second)
            gates[m, q] = 1.0 / (1.0 + jnp.exp(-z))

    for m in range(2):
        pltpu.make_async_copy(r_recv.at[m], r_recv.at[m], r_sem.at[m, 1]).wait()
        parts = from_chunks(r_recv.at[m])
        outputs = []
        for k in range(4):
            mixed = dot(mix[m], parts[k].astype(BF16)).astype(BF16).astype(F32)
            y = (x_all[k] + mixed * gates[m, k]).astype(BF16).astype(F32)
            sums[m * 4 + k:m * 4 + k + 1, :] = jnp.sum(y, axis=0, keepdims=True)
            outputs.append(y)
        if m == 0:
            to_chunks(outputs, y_send)
            keep_own(y_send, y_recv, y_sem)
            send_part(y_send, y_recv, y_sem, 0, n_c // 8 * 3)

    stage = (sums, buf_y, send_y, recv_y, at.y_peer, at.y, at.n_y)
    pending += spread_out(*stage)
    send_part(y_send, y_recv, y_sem, n_c // 8 * 3, n_c // 8 * 5)
    gathered(*stage)
    own_y[...] = total_of(buf_y, at.n_y)
    stage = (own_y, buf_w, send_w, recv_w, at.w_peer, at.w, at.n_w)
    pending += spread_out(*stage)
    send_part(y_send, y_recv, y_sem, n_c // 8 * 5, n_c // 8 * 6)
    gathered(*stage)
    own_w[...] = total_of(buf_w, at.n_w) / seq_len
    stage = (own_w, buf_d, send_d, recv_d, at.d_peer, at.dp, n_d)
    pending += spread_out(*stage)
    send_part(y_send, y_recv, y_sem, n_c // 8 * 6, n_c // 8 * 7)
    gathered(*stage)
    local = []
    reps = n_d // 4
    for m in range(2):
        mine = (iota((8, 1), 0) == m * 4 + at.dp // reps).astype(F32)
        model = (iota((8, 1), 0) // 4 == m).astype(F32)
        rows, norms = [], []
        for n in range(n_d):
            pooled = buf_d[n]
            rows.append(jnp.sum(pooled * mine, axis=0, keepdims=True))
            square = jnp.sum(pooled * pooled * model, axis=0, keepdims=True)
            norms.append(jnp.sum(square, axis=1, keepdims=True))
        norm = lax.rsqrt(jnp.concatenate(norms, axis=0) / (4 * width) + 1e-06)
        head = head_refs[m][...].astype(F32)
        slot = iota((width, 1), 0) // (width // reps)
        head = jnp.where(slot == lax.rem(at.dp, reps), jnp.concatenate([head] * reps, axis=0), 0.0)
        local.append(jnp.dot(jnp.concatenate(rows, axis=0) * norm, head,
                             precision=lax.Precision.HIGHEST, preferred_element_type=F32))
    own_l[...] = jnp.concatenate(local, axis=1)
    stage = (own_l, buf_l, send_l, recv_l, at.d_peer, at.dp, n_d)
    pending += spread_out(*stage)
    send_part(y_send, y_recv, y_sem, n_c // 8 * 7, n_c - 1)
    gathered(*stage)
    logits = total_of(buf_l, n_d)
    classes = logits.shape[1] // 2
    row = iota((n_d, 1), 0)
    target = jnp.zeros((n_d, 1), jnp.int32)
    for n in range(n_d):
        target = jnp.where(row == n, target_ref[n], target)
    chosen = iota((n_d, classes), 1) == target
    losses = []
    for part in (logits[:, :classes], logits[:, classes:]):
        top = jnp.max(part, axis=1, keepdims=True)
        summed = jnp.log(jnp.sum(jnp.exp(part - top), axis=1, keepdims=True)) + top
        losses.append(summed - jnp.sum(jnp.where(chosen, part, 0.0), axis=1, keepdims=True))
    scores = losses[0] - losses[1]
    for n in range(n_d):
        score_ref[n] = jnp.sum(jnp.where(row == n, scores, 0.0))
    for k in range(candidate_ref.shape[0]):
        picked_ref[k] = jnp.sum(jnp.where(row == candidate_ref[k], scores, 0.0))

    pltpu.make_async_copy(y_recv, y_recv, y_sem.at[1]).wait()
    parts = from_chunks(y_recv)
    for k in range(4):
        out_ref[:, k * width:(k + 1) * width] = parts[k].astype(BF16)

    def sent(view, sem):
        pltpu.make_async_copy(view, view, sem).wait()

    sent(xa_send.at[pl.ds(0, n_c - 1)], xa_sem.at[0])
    for buf, sem in ((xb_send, xb_sem.at[0]), (r_send.at[0], r_sem.at[0, 0]),
                     (r_send.at[1], r_sem.at[1, 0]), (y_send, y_sem.at[0])):
        sent(buf.at[pl.ds(0, n_c // 2 - 1)], sem)
        sent(buf.at[0, 0], sem)
    for copy in pending:
        copy.wait_send()


def layer_call(ids, target, candidates, table, online, frozen, seq_len):
    n_d, n_c = lax.axis_size("dp"), lax.axis_size("ctx")
    n_x = 4 if n_c == 64 else n_c // 2
    n_w = 2 * n_x
    n_y = n_c // n_w
    feats, vocab = table.shape
    block = online[0].shape[1]
    depth, width = online[2].shape[2:]
    wide = -(-(width // 4) // 128) * 128
    n_l = -(-vocab // (2 * block)) * 2
    classes = online[4].shape[1]
    dma = pltpu.SemaphoreType.DMA
    found = (n_c, 2 * feats, block // 2)
    chunks = (n_c // 2, 2, 16, width)
    vmem, smem = pl.BlockSpec(memory_space=pltpu.VMEM), pl.BlockSpec(memory_space=pltpu.SMEM)
    return pl.pallas_call(
        functools.partial(layer_kernel, (n_d, n_c, seq_len)),
        out_shape=(jax.ShapeDtypeStruct((block, 4 * width), BF16),
                   jax.ShapeDtypeStruct((n_d,), F32),
                   jax.ShapeDtypeStruct(candidates.shape, F32)),
        in_specs=[vmem, smem, smem] + [vmem] * 11,
        out_specs=(vmem, smem, smem),
        scratch_shapes=[
            pltpu.VMEM((n_l * feats, block), BF16),
            pltpu.VMEM(found, BF16), pltpu.VMEM(found, BF16),
            pltpu.VMEM(chunks, BF16), pltpu.VMEM(chunks, BF16),
            pltpu.VMEM((2, n_c * feats, block // 2), F32),
            pltpu.VMEM((4, block, width), F32),
            pltpu.VMEM((2,) + chunks, BF16), pltpu.VMEM((2,) + chunks, BF16),
            pltpu.VMEM(chunks, BF16), pltpu.VMEM(chunks, BF16),
            pltpu.VMEM((2, 2, 4, depth * n_d, width), BF16),
            pltpu.VMEM((2, 4, block, width), F32),
            pltpu.VMEM((2, block, block), BF16),
            pltpu.VMEM((width, 4 * wide), BF16), pltpu.VMEM((4 * wide, width), BF16),
            pltpu.VMEM((4, block, 4 * wide), BF16),
            pltpu.VMEM((8, width), F32),
            pltpu.VMEM((n_y, 8, width), F32), pltpu.VMEM((n_w, 8, width), F32),
            pltpu.VMEM((n_d, 8, width), F32), pltpu.VMEM((n_d, n_d, 2 * classes), F32),
            pltpu.VMEM((8, width), F32), pltpu.VMEM((8, width), F32),
            pltpu.VMEM((n_d, 2 * classes), F32),
            dma((2,)), dma((2,)), dma((2, 2)), dma((2,)),
            dma((2, 3)), dma((2, 3)), dma((2, 3, max(n_x - 1, 1))), dma((2, 3, max(n_x - 1, 1))),
            dma((2, 4)), dma((2, 4)), dma((2,)),
            dma((n_y,)), dma((n_y,)), dma((n_w,)), dma((n_w,)),
            dma((n_d,)), dma((n_d,)), dma((n_d,)), dma((n_d,)),
        ],
        compiler_params=pltpu.CompilerParams(
            collective_id=1, has_side_effects=True, vmem_limit_bytes=56 * 1024 * 1024),
        name="layer",
    )(ids, target, candidates, table, *online, *frozen)


def body(
    token_ids,
    target_ids,
    candidates,
    embed_table,
    online_blocks,
    online_across,
    online_channel,
    online_gain,
    online_head,
    ref_blocks,
    ref_across,
    ref_channel,
    ref_gain,
    ref_head,
):
    return layer_call(
        token_ids,
        target_ids,
        candidates,
        embed_table,
        (online_blocks, online_across, online_channel, online_gain, online_head),
        (ref_blocks, ref_across, ref_channel, ref_gain, ref_head),
        token_ids.shape[1],
    )


def solution(mesh):
    in_specs = (
        P("dp", None),
        P(),
        P(),
        P("ctx", None),
        P("ctx", None, None),
        P("ctx", None, None),
        P(None, None, "dp", None),
        P(),
        P("dp", None),
        P("ctx", None, None),
        P("ctx", None, None),
        P(None, None, "dp", None),
        P(),
        P("dp", None),
    )
    out_specs = (P(("dp", "ctx"), None), P(), P())
    return jax.shard_map(body, mesh=mesh, in_specs=in_specs, out_specs=out_specs, check_vma=False)
```

```python
import functools
import jax
import jax.numpy as jnp
from jax import lax
from jax.experimental import pallas as pl
from jax.experimental.pallas import tpu as pltpu
from jax.sharding import PartitionSpec as P

MESH = pl.DeviceIdType.MESH
F32 = jnp.float32
BF16 = jnp.bfloat16
HALF_TILE = 4


def dot(a, b):
    return jnp.dot(a, b, preferred_element_type=F32)


def iota(shape, axis):
    return lax.broadcasted_iota(jnp.int32, shape, axis)


class Place:
    def __init__(self, n_d, n_c):
        self.n_d, self.n_c = n_d, n_c
        self.n_x = 4 if n_c == 64 else n_c // 2
        self.n_y = n_c // (2 * self.n_x)
        self.n_w = 2 * self.n_x
        self.z_lo_size = n_d // 2
        self.z_size = 2 * self.z_lo_size
        self.dp, self.ctx = lax.axis_index("dp"), lax.axis_index("ctx")
        self.y, self.w = self.ctx // self.n_w, lax.rem(self.ctx, self.n_w)
        self.z_hi, self.x = self.w // self.n_x, lax.rem(self.w, self.n_x)
        self.z_lo, self.core = self.dp // 2, lax.rem(self.dp, 2)
        self.z = self.z_hi * self.z_lo_size + self.z_lo

    def ctx_at(self, o):
        step_z, rest = lax.rem(o, 2), o // 2
        step_y = lax.rem(rest * 3, self.n_y)
        step_x = lax.rem(rest // self.n_y + lax.rem(rest, self.n_y), self.n_x)
        y = lax.rem(self.y + step_y, self.n_y)
        z_hi = lax.rem(self.z_hi + step_z, 2)
        x = lax.rem(self.x + step_x, self.n_x)
        return y * self.n_w + z_hi * self.n_x + x

    def z_at(self, step):
        z = lax.rem(self.z + step, self.z_size)
        dp = lax.rem(z, self.z_lo_size) * 2 + self.core
        ctx = self.y * self.n_w + (z // self.z_lo_size) * self.n_x + self.x
        return dp, ctx

    def x_peer(self, o):
        x = lax.rem(self.x + o, self.n_x)
        return (self.dp, self.y * self.n_w + self.z_hi * self.n_x + x)

    def y_peer(self, o):
        return (self.dp, lax.rem(self.y + o, self.n_y) * self.n_w + self.w)

    def w_peer(self, o):
        return (self.dp, self.y * self.n_w + lax.rem(self.w + o, self.n_w))

    def d_peer(self, o):
        return (lax.rem(self.dp + o, self.n_d), self.ctx)


def remote(src, dst, send, recv, device):
    return pltpu.make_async_remote_copy(
        src_ref=src, dst_ref=dst, send_sem=send, recv_sem=recv,
        device_id=device, device_id_type=MESH)


def spread_out(own, buf, send, recv, peer, me, count):
    copies = []
    for o in range(1, count):
        copy = remote(own, buf.at[me], send.at[o], recv.at[me], peer(o))
        copy.start()
        copies.append(copy)
    buf[me] = own[...]
    return copies


def gathered(own, buf, send, recv, peer, me, count):
    for o in range(1, count):
        slot = lax.rem(me + o, count)
        remote(own, buf.at[slot], send.at[o], recv.at[slot], peer(o)).wait_recv()


def total_of(buf, count):
    total = buf[0]
    for j in range(1, count):
        total = total + buf[j]
    return total


def to_chunks(parts, ref):
    rows, width = parts[0].shape
    tiles = [p.reshape(rows // 8, 8, width) for p in parts]
    rolled = [pltpu.roll(t, HALF_TILE, 1) for t in tiles]
    upper = iota((1, 8, 1), 1) < HALF_TILE
    even = [jnp.where(upper, tiles[i], rolled[i + 1]) for i in (0, 2)]
    odd = [jnp.where(upper, rolled[i], tiles[i + 1]) for i in (0, 2)]
    ref[:, 0] = jnp.concatenate(even, axis=1).astype(BF16)
    ref[:, 1] = jnp.concatenate(odd, axis=1).astype(BF16)


def from_chunks(ref):
    even, odd = ref[:, 0].astype(F32), ref[:, 1].astype(F32)
    rows, width = even.shape[0] * 8, even.shape[2]
    upper = iota((1, 8, 1), 1) < HALF_TILE
    parts = []
    for i in (0, 1):
        e, o = even[:, 8 * i:8 * i + 8], odd[:, 8 * i:8 * i + 8]
        parts.append(jnp.where(upper, e, pltpu.roll(o, HALF_TILE, 1)).reshape(rows, width))
        parts.append(jnp.where(upper, pltpu.roll(e, HALF_TILE, 1), o).reshape(rows, width))
    return parts


def layer_kernel(
    dims, ids_ref, target_ref, candidate_ref, table_ref,
    online_blocks, online_across, online_channel, online_gain, online_head,
    frozen_blocks, frozen_across, frozen_channel, frozen_gain, frozen_head,
    out_ref, score_ref, picked_ref,
    tall, xa_send, xa_recv, xb_send, xb_recv, flipped, x_all, r_send, r_recv, y_send, y_recv,
    factors, gates, mix, spread, gather, padded, sums,
    buf_y, buf_w, buf_d, buf_l, own_y, own_w, own_l,
    xa_sem, xb_sem, r_sem, y_sem, f_send, f_recv, e_send, e_recv, g_send, g_recv, local_sem,
    send_y, recv_y, send_w, recv_w, send_d, recv_d, send_l, recv_l,
):
    n_d, n_c, seq_len = dims
    at = Place(n_d, n_c)
    blocks_refs = (online_blocks, frozen_blocks)
    across_refs = (online_across, frozen_across)
    channel_refs = (online_channel, frozen_channel)
    gain_refs = (online_gain, frozen_gain)
    head_refs = (online_head, frozen_head)
    feats, vocab = table_ref.shape
    block = online_blocks.shape[1]
    half = block // 2
    depth, width = online_channel.shape[2:]
    quarter = width // 4
    wide = gather.shape[0] // 4
    n_l = tall.shape[0] // feats
    n_z = at.z_size
    group = online_across.shape[0]

    barrier = pltpu.get_barrier_semaphore()

    def greet(o, carry):
        pl.semaphore_signal(barrier, inc=1, device_id=(at.dp, at.ctx_at(o)), device_id_type=MESH)
        return carry

    lax.fori_loop(1, n_c, greet, 0)
    for o in range(1, n_d):
        pl.semaphore_signal(barrier, inc=1, device_id=at.d_peer(o), device_id_type=MESH)
    for step in (1, 2, n_z - 2, n_z - 1):
        pl.semaphore_signal(barrier, inc=1, device_id=at.z_at(step), device_id_type=MESH)

    def tall_pair(i, carry):
        start = pl.multiple_of(i * 2 * block, 2 * block)
        pair = table_ref[:, pl.ds(start, 2 * block)].astype(F32)
        tall[pl.ds(pl.multiple_of(i * 2 * feats, 2 * feats), 2 * feats), :] = jnp.concatenate(
            [pair[:, :block], pair[:, block:]], axis=0).astype(BF16)
        return carry

    full = vocab // (2 * block)
    lax.fori_loop(0, full, tall_pair, 0)
    if full * 2 < n_l:
        left = table_ref[:, full * 2 * block:].astype(F32)
        left = jnp.concatenate(
            [left, jnp.zeros((feats, 2 * block - left.shape[1]), F32)], axis=1)
        tall[full * 2 * feats:, :] = jnp.concatenate(
            [left[:, :block], left[:, block:]], axis=0).astype(BF16)

    n_k = 4 // at.n_x

    def shard(m, dp, x=None):
        rows = pl.ds(pl.multiple_of(dp * depth, depth), depth)
        if x is None:
            return factors.at[m, :, :, rows, :]
        return factors.at[m, :, pl.ds(x * n_k, n_k), rows, :]

    steps = (1, n_z - 1, lax.rem(2 + at.core * (n_z - 4), n_z))
    sources = [at.z_at(n_z - step)[0] for step in steps]
    pending = []
    own_factors = []
    for m in range(2):
        copy = pltpu.make_async_copy(channel_refs[m], shard(m, at.dp), local_sem.at[m])
        copy.start()
        own_factors.append(copy)

    l_step = 8 if n_l % 8 == 0 else 2
    per_step = 2

    def send_found(i):
        dest = at.ctx_at(n_c - 1 - i)

        @pl.when(i < n_c - 1)
        def _():
            remote(xa_send.at[dest], xa_recv.at[at.ctx], xa_sem.at[0], xa_sem.at[1],
                   (at.dp, dest)).start()

        @pl.when(i == n_c - 1)
        def _():
            pltpu.make_async_copy(xa_send.at[dest], xa_recv.at[at.ctx], xa_sem.at[1]).start()

    def send_early(i, carry):
        send_found(i)
        return carry

    def lookup(i, carry, sending=True):
        dests = [at.ctx_at(n_c - 1 - (i * per_step + j)) for j in range(per_step)]
        ids = jnp.concatenate(
            [ids_ref[:, pl.ds(pl.multiple_of(d * block, block), block)] for d in dests], axis=1)
        low, high = lax.rem(ids, block), ids // block
        hot = jnp.where(iota((block, per_step * block), 0) == low, 1.0, 0.0).astype(BF16)
        found = jnp.zeros((feats, per_step * block), F32)
        for start in range(0, n_l, l_step):
            picked = dot(tall[start * feats:(start + l_step) * feats, :], hot)
            for l in range(l_step):
                found = jnp.where(high == start + l, picked[l * feats:(l + 1) * feats], found)
        for j, dest in enumerate(dests):
            mine = found[:, j * block:(j + 1) * block]
            xa_send[dest] = jnp.concatenate([mine[:, :half], mine[:, half:]], axis=0).astype(BF16)

            if sending:
                send_found(i * per_step + j)

        return carry

    def unpack():
        pltpu.make_async_copy(xa_recv, xa_recv, xa_sem.at[1]).wait()

        def flip(i, carry):
            both = xa_recv[i].astype(F32)
            start = pl.multiple_of(i * feats, feats)
            flipped[0, pl.ds(start, feats), :] = both[:feats]
            flipped[1, pl.ds(start, feats), :] = both[feats:]
            return carry

        lax.fori_loop(0, n_c, flip, 0)
        for i in range(2):
            for k in range(4):
                x_all[k, i * half:(i + 1) * half, :] = flipped[i, k * width:(k + 1) * width, :].T

    def norm_scale():
        square = jnp.zeros((block, 1), F32)
        for k in range(4):
            square = square + jnp.sum(x_all[k] * x_all[k], axis=1, keepdims=True)
        return lax.rsqrt(square / (4 * width) + 1e-06)

    def normed(m, k, scale):
        gain = gain_refs[m][k * width:(k + 1) * width].astype(F32).reshape(1, width)
        return (x_all[k] * scale * gain).astype(BF16)

    def send_part(send, recv, sems, first, last):
        def one(i, carry):
            dest = at.ctx_at(n_c - 1 - i)
            remote(send.at[dest // 2, lax.rem(dest, 2)],
                   recv.at[at.ctx // 2, lax.rem(at.ctx, 2)],
                   sems.at[0], sems.at[1], (at.dp, dest)).start()
            return carry

        lax.fori_loop(first, last, one, 0)

    def keep_own(send, recv, sems):
        pltpu.make_async_copy(send.at[at.ctx // 2, lax.rem(at.ctx, 2)],
                              recv.at[at.ctx // 2, lax.rem(at.ctx, 2)], sems.at[1]).start()

    def send_chunks(parts, send, recv, sems):
        to_chunks(parts, send)
        send_part(send, recv, sems, 0, n_c - 1)
        keep_own(send, recv, sems)

    n_steps = n_c // per_step
    early = n_steps // 2

    lax.fori_loop(0, early, functools.partial(lookup, sending=False), 0)
    pl.semaphore_wait(barrier, n_c - 1 + n_d - 1 + 4)
    lax.fori_loop(0, early * per_step, send_early, 0)
    lax.fori_loop(early, n_steps, lookup, 0)

    for m in range(2):
        for j, step in enumerate(steps):
            copy = remote(channel_refs[m].at[:, pl.ds(at.x * n_k, n_k)], shard(m, at.dp, at.x),
                          f_send.at[m, j], f_recv.at[m, j], at.z_at(step))
            copy.start()
            pending.append(copy)

    unpack()
    send_chunks([x_all[k] for k in range(4)], xb_send, xb_recv, xb_sem)
    for m in range(2):
        for j, source in enumerate(sources):
            remote(shard(m, source, at.x), shard(m, source, at.x), f_send.at[m, j],
                   f_recv.at[m, j], at.z_at(steps[j])).wait_recv()
            for o in range(1, at.n_x):
                copy = remote(shard(m, source, at.x), shard(m, source, at.x),
                              e_send.at[m, j, o - 1], e_recv.at[m, j, o - 1], at.x_peer(o))
                copy.start()
                pending.append(copy)

    scale = norm_scale()
    def within(m):
        send_chunks([dot(blocks_refs[m][0], normed(m, k, scale)) for k in range(4)],
                    r_send.at[m], r_recv.at[m], r_sem.at[m])

    within(0)

    other = at.dp + 1 - 2 * at.core
    sibling = (other, at.ctx)
    for m in range(2):
        own_factors[m].wait()
        for j, source in enumerate([at.dp] + sources):
            if j:
                for o in range(1, at.n_x):
                    part = shard(m, source, lax.rem(at.x + at.n_x - o, at.n_x))
                    remote(part, part, e_send.at[m, j - 1, o - 1], e_recv.at[m, j - 1, o - 1],
                           at.x_peer(o)).wait_recv()
            copy = remote(shard(m, source), shard(m, source), g_send.at[m, j], g_recv.at[m, j],
                          sibling)
            copy.start()
            pending.append(copy)

    within(1)


    tall_one = jnp.where(iota((block, n_c), 0) // group == iota((block, n_c), 1), 1.0, 0.0)
    wide_one = jnp.where(iota((n_c, block), 1) // group == iota((n_c, block), 0), 1.0, 0.0)
    row_b, col_b = lax.rem(iota((block, block), 0), group), lax.rem(iota((block, block), 1), group)
    for m in range(2):
        total = jnp.zeros((block, block), F32)
        for b in range(group):
            piece = dot(dot(tall_one.astype(BF16), across_refs[m][b]).astype(BF16),
                        wide_one.astype(BF16))
            total = jnp.where((row_b == b) & (col_b == b), piece, total)
        mix[m] = total.astype(BF16)
    place, lane = iota((width, 4 * wide), 0), iota((width, 4 * wide), 1)
    inner = lax.rem(lane, wide)
    spread[...] = jnp.where(
        (place == (lane // wide) * quarter + inner) & (inner < quarter), 1.0, 0.0).astype(BF16)
    place, lane = iota((4 * wide, width), 0), iota((4 * wide, width), 1)
    inner = lax.rem(place, wide)
    gather[...] = jnp.where(
        (lane == inner * 4 + place // wide) & (inner < quarter), 1.0, 0.0).astype(BF16)

    pltpu.make_async_copy(xb_recv, xb_recv, xb_sem.at[1]).wait()
    parts = from_chunks(xb_recv)
    for k in range(4):
        x_all[k] = parts[k]
    scale = norm_scale()
    for m in range(2):
        for j in range(4):
            source = (at.dp if j == 0 else sources[j - 1]) + 1 - 2 * at.core
            remote(shard(m, source), shard(m, source), g_send.at[m, j], g_recv.at[m, j],
                   sibling).wait_recv()
        for k in range(4):
            first = dot(normed(m, k, scale), factors[m, 0, k]).astype(BF16)
            first = dot(first, spread[...]).astype(BF16)
            for q in range(4):
                padded[q, :, k * wide:(k + 1) * wide] = first[:, q * wide:(q + 1) * wide]
        for q in range(4):
            second = dot(gather[...], factors[m, 1, q]).astype(BF16)
            z = dot(padded[q], second)
            gates[m, q] = 1.0 / (1.0 + jnp.exp(-z))

    for m in range(2):
        pltpu.make_async_copy(r_recv.at[m], r_recv.at[m], r_sem.at[m, 1]).wait()
        parts = from_chunks(r_recv.at[m])
        outputs = []
        for k in range(4):
            mixed = dot(mix[m], parts[k].astype(BF16)).astype(BF16).astype(F32)
            y = (x_all[k] + mixed * gates[m, k]).astype(BF16).astype(F32)
            sums[m * 4 + k:m * 4 + k + 1, :] = jnp.sum(y, axis=0, keepdims=True)
            outputs.append(y)
        if m == 0:
            to_chunks(outputs, y_send)
            keep_own(y_send, y_recv, y_sem)
            send_part(y_send, y_recv, y_sem, 0, n_c // 8 * 3)

    stage = (sums, buf_y, send_y, recv_y, at.y_peer, at.y, at.n_y)
    pending += spread_out(*stage)
    send_part(y_send, y_recv, y_sem, n_c // 8 * 3, n_c // 8 * 5)
    gathered(*stage)
    own_y[...] = total_of(buf_y, at.n_y)
    stage = (own_y, buf_w, send_w, recv_w, at.w_peer, at.w, at.n_w)
    pending += spread_out(*stage)
    send_part(y_send, y_recv, y_sem, n_c // 8 * 5, n_c // 8 * 6)
    gathered(*stage)
    own_w[...] = total_of(buf_w, at.n_w) / seq_len
    stage = (own_w, buf_d, send_d, recv_d, at.d_peer, at.dp, n_d)
    pending += spread_out(*stage)
    send_part(y_send, y_recv, y_sem, n_c // 8 * 6, n_c // 8 * 7)
    gathered(*stage)
    local = []
    reps = n_d // 4
    for m in range(2):
        mine = (iota((8, 1), 0) == m * 4 + at.dp // reps).astype(F32)
        model = (iota((8, 1), 0) // 4 == m).astype(F32)
        rows, norms = [], []
        for n in range(n_d):
            pooled = buf_d[n]
            rows.append(jnp.sum(pooled * mine, axis=0, keepdims=True))
            square = jnp.sum(pooled * pooled * model, axis=0, keepdims=True)
            norms.append(jnp.sum(square, axis=1, keepdims=True))
        norm = lax.rsqrt(jnp.concatenate(norms, axis=0) / (4 * width) + 1e-06)
        head = head_refs[m][...].astype(F32)
        slot = iota((width, 1), 0) // (width // reps)
        head = jnp.where(slot == lax.rem(at.dp, reps), jnp.concatenate([head] * reps, axis=0), 0.0)
        local.append(jnp.dot(jnp.concatenate(rows, axis=0) * norm, head,
                             precision=lax.Precision.HIGHEST, preferred_element_type=F32))
    own_l[...] = jnp.concatenate(local, axis=1)
    stage = (own_l, buf_l, send_l, recv_l, at.d_peer, at.dp, n_d)
    pending += spread_out(*stage)
    send_part(y_send, y_recv, y_sem, n_c // 8 * 7, n_c - 1)
    gathered(*stage)
    logits = total_of(buf_l, n_d)
    classes = logits.shape[1] // 2
    row = iota((n_d, 1), 0)
    target = jnp.zeros((n_d, 1), jnp.int32)
    for n in range(n_d):
        target = jnp.where(row == n, target_ref[n], target)
    chosen = iota((n_d, classes), 1) == target
    losses = []
    for part in (logits[:, :classes], logits[:, classes:]):
        top = jnp.max(part, axis=1, keepdims=True)
        summed = jnp.log(jnp.sum(jnp.exp(part - top), axis=1, keepdims=True)) + top
        losses.append(summed - jnp.sum(jnp.where(chosen, part, 0.0), axis=1, keepdims=True))
    scores = losses[0] - losses[1]
    for n in range(n_d):
        score_ref[n] = jnp.sum(jnp.where(row == n, scores, 0.0))
    for k in range(candidate_ref.shape[0]):
        picked_ref[k] = jnp.sum(jnp.where(row == candidate_ref[k], scores, 0.0))

    pltpu.make_async_copy(y_recv, y_recv, y_sem.at[1]).wait()
    parts = from_chunks(y_recv)
    for k in range(4):
        out_ref[:, k * width:(k + 1) * width] = parts[k].astype(BF16)

    def sent(view, sem):
        pltpu.make_async_copy(view, view, sem).wait()

    sent(xa_send.at[pl.ds(0, n_c - 1)], xa_sem.at[0])
    for buf, sem in ((xb_send, xb_sem.at[0]), (r_send.at[0], r_sem.at[0, 0]),
                     (r_send.at[1], r_sem.at[1, 0]), (y_send, y_sem.at[0])):
        sent(buf.at[pl.ds(0, n_c // 2 - 1)], sem)
        sent(buf.at[0, 0], sem)
    for copy in pending:
        copy.wait_send()


def layer_call(ids, target, candidates, table, online, frozen, seq_len):
    n_d, n_c = lax.axis_size("dp"), lax.axis_size("ctx")
    n_x = 4 if n_c == 64 else n_c // 2
    n_w = 2 * n_x
    n_y = n_c // n_w
    feats, vocab = table.shape
    block = online[0].shape[1]
    depth, width = online[2].shape[2:]
    wide = -(-(width // 4) // 128) * 128
    n_l = -(-vocab // (2 * block)) * 2
    classes = online[4].shape[1]
    dma = pltpu.SemaphoreType.DMA
    found = (n_c, 2 * feats, block // 2)
    chunks = (n_c // 2, 2, 16, width)
    vmem, smem = pl.BlockSpec(memory_space=pltpu.VMEM), pl.BlockSpec(memory_space=pltpu.SMEM)
    return pl.pallas_call(
        functools.partial(layer_kernel, (n_d, n_c, seq_len)),
        out_shape=(jax.ShapeDtypeStruct((block, 4 * width), BF16),
                   jax.ShapeDtypeStruct((n_d,), F32),
                   jax.ShapeDtypeStruct(candidates.shape, F32)),
        in_specs=[vmem, smem, smem] + [vmem] * 11,
        out_specs=(vmem, smem, smem),
        scratch_shapes=[
            pltpu.VMEM((n_l * feats, block), BF16),
            pltpu.VMEM(found, BF16), pltpu.VMEM(found, BF16),
            pltpu.VMEM(chunks, BF16), pltpu.VMEM(chunks, BF16),
            pltpu.VMEM((2, n_c * feats, block // 2), F32),
            pltpu.VMEM((4, block, width), F32),
            pltpu.VMEM((2,) + chunks, BF16), pltpu.VMEM((2,) + chunks, BF16),
            pltpu.VMEM(chunks, BF16), pltpu.VMEM(chunks, BF16),
            pltpu.VMEM((2, 2, 4, depth * n_d, width), BF16),
            pltpu.VMEM((2, 4, block, width), F32),
            pltpu.VMEM((2, block, block), BF16),
            pltpu.VMEM((width, 4 * wide), BF16), pltpu.VMEM((4 * wide, width), BF16),
            pltpu.VMEM((4, block, 4 * wide), BF16),
            pltpu.VMEM((8, width), F32),
            pltpu.VMEM((n_y, 8, width), F32), pltpu.VMEM((n_w, 8, width), F32),
            pltpu.VMEM((n_d, 8, width), F32), pltpu.VMEM((n_d, n_d, 2 * classes), F32),
            pltpu.VMEM((8, width), F32), pltpu.VMEM((8, width), F32),
            pltpu.VMEM((n_d, 2 * classes), F32),
            dma((2,)), dma((2,)), dma((2, 2)), dma((2,)),
            dma((2, 3)), dma((2, 3)), dma((2, 3, max(n_x - 1, 1))), dma((2, 3, max(n_x - 1, 1))),
            dma((2, 4)), dma((2, 4)), dma((2,)),
            dma((n_y,)), dma((n_y,)), dma((n_w,)), dma((n_w,)),
            dma((n_d,)), dma((n_d,)), dma((n_d,)), dma((n_d,)),
        ],
        compiler_params=pltpu.CompilerParams(
            collective_id=1, has_side_effects=True, vmem_limit_bytes=56 * 1024 * 1024),
        name="layer",
    )(ids, target, candidates, table, *online, *frozen)


def body(
    token_ids,
    target_ids,
    candidates,
    embed_table,
    online_blocks,
    online_across,
    online_channel,
    online_gain,
    online_head,
    ref_blocks,
    ref_across,
    ref_channel,
    ref_gain,
    ref_head,
):
    return layer_call(
        token_ids,
        target_ids,
        candidates,
        embed_table,
        (online_blocks, online_across, online_channel, online_gain, online_head),
        (ref_blocks, ref_across, ref_channel, ref_gain, ref_head),
        token_ids.shape[1],
    )


def solution(mesh):
    in_specs = (
        P("dp", None),
        P(),
        P(),
        P("ctx", None),
        P("ctx", None, None),
        P("ctx", None, None),
        P(None, None, "dp", None),
        P(),
        P("dp", None),
        P("ctx", None, None),
        P("ctx", None, None),
        P(None, None, "dp", None),
        P(),
        P("dp", None),
    )
    out_specs = (P(("dp", "ctx"), None), P(), P())
    return jax.shard_map(body, mesh=mesh, in_specs=in_specs, out_specs=out_specs, check_vma=False)
```
